256 devices in a mesh: dp: 16 (over y_hi, x, core), mp: 16 (over z, y_lo).
Axes of the slice: x: 4, y: 4 (y_hi: 2, y_lo: 2; y = y_hi * 2 + y_lo), z: 8, core: 2. Of those that a mesh axis runs over, the one named last changes fastest.
Arguments:
- grid_fields: bfloat16 [16, 16384, 128], P('dp', 'mp'), may hold values from -2.09375 to 2.09375
- cotangent: bfloat16 [16, 2048, 1024], P('dp', 'mp'), may hold values from -6 to 6
- encoder_source: int32 [16, 2048], replicated, may hold values from 0 to 16383
- encoder_target: int32 [16, 2048], replicated, may hold values from 0 to 127
- encoder_count: int32 [16], replicated, may hold values from 512 to 2048, as said below
- mesh_source: int32 [16, 512], replicated, may hold values from 0 to 2047
- mesh_target: int32 [16, 512], replicated, may hold values from 0 to 127
- mesh_count: int32 [16], replicated, may hold values from 256 to 512, as said below
- w_encoder: bfloat16 [128, 1024], replicated, may hold values from -0.5 to 0.5
- w_query: bfloat16 [1024, 1024], replicated, may hold values from -0.1875 to 0.1875
- w_key: bfloat16 [1024, 1024], replicated, may hold values from -0.1875 to 0.1875
- w_value: bfloat16 [1024, 1024], replicated, may hold values from -0.1875 to 0.1875
- w_output: bfloat16 [1024, 1024], replicated, may hold values from -0.1875 to 0.1875
Outputs:
- grad_query: float32 [1024, 1024], P('mp')
- grad_key: float32 [1024, 1024], P('mp')
- grad_value: float32 [1024, 1024], P('mp')
- grad_output: float32 [1024, 1024], P('mp')
- grad_encoder: float32 [128, 1024], P('mp')
The draws below stay inside these ranges and needn't reach their ends.
Inputs may be any that keep to these rules, and one draw needn't show every extreme that they name: `encoder_count`: live encoder slots of each block; a run of 1 neighbouring blocks is dense and one block is full. `mesh_count`: live processor slots of each block; one block is full.
All inputs are finite; a program needn't handle non-finite values.
Results may differ from the reference program's by a relative error of at most 0.014.
The reference program's roundings to bfloat16 on the way count: a program that leaves them out, or rounds other values in their place, can miss the bound.
Values may be sent and summed in bfloat16 or wider, within the bound.
No kernel may reach another device: no remote copies, remote signals or barrier semaphores. Data moves between devices by JAX's collectives and lax.ppermute only.
A program may use at most 128 MiB of HBM per device.

```python
import math
import jax
import jax.numpy as jnp
from jax import lax

D = 1024
HEADS = 16
C = 128
BLOCK = 128
ECAP = 2048
PCAP = 512
HD = 64
NODES = 2048
GRID = 16384
NBLK = 16
BLK_DEV = 1
SAMPLES = 16


def draw_encoder_count(key, part):
    key = jax.random.fold_in(key, 11)
    first_key, second_key, third_key = jax.random.split(key, 3)
    position = jnp.arange(NBLK, dtype=jnp.int32)
    sparse = jax.random.randint(first_key, (NBLK,), ECAP // 4, ECAP // 2 + 1)
    dense = jax.random.randint(second_key, (NBLK,), 3 * ECAP // 4, ECAP + 1)
    nest_start = jax.random.randint(third_key, (), 0, NBLK - BLK_DEV + 1)
    inside = (position >= nest_start) & (position < nest_start + BLK_DEV)
    counts = jnp.where(inside, dense, sparse)
    counts = jnp.where(position == nest_start, ECAP, counts)
    return counts.astype(jnp.int32)


def draw_mesh_count(key, part):
    key = jax.random.fold_in(key, 23)
    first_key, second_key = jax.random.split(key, 2)
    position = jnp.arange(NBLK, dtype=jnp.int32)
    counts = jax.random.randint(first_key, (NBLK,), PCAP // 2, PCAP + 1)
    fullest = jax.random.randint(second_key, (), 0, NBLK)
    counts = jnp.where(position == fullest, PCAP, counts)
    return counts.astype(jnp.int32)


def with_ends(values, stream_key, low, top_value):
    place = [jax.random.randint(jax.random.fold_in(stream_key, axis), (), 0, length) for axis, length in enumerate(values.shape)]
    widest = values.shape.index(max(values.shape))
    next_to = place[:widest] + [(place[widest] + 1) % values.shape[widest]] + place[widest + 1:]
    return values.at[tuple(place)].set(low).at[tuple(next_to)].set(top_value)


def raised(result, stream_key, source, target, blocks, factor):
    owner, partner = [(jnp.arange(result.shape[dim]) // (result.shape[dim] // blocks)).reshape([-1 if axis == dim else 1 for axis in range(result.ndim)]) for dim in (source, target)]
    chosen = jax.random.permutation(stream_key, blocks)[partner]
    strong = (owner == chosen) | (owner == (partner + blocks // 2) % blocks)
    return jnp.where(strong, factor * result, result)


def levels(rng, shape, cuts, smallest, high):
    def one(dim, shards_of):
        draws = jax.random.uniform(jax.random.fold_in(jax.random.fold_in(rng, 6), dim), (shards_of,), jnp.float32, smallest / len(cuts), high / len(cuts))
        return jnp.repeat(jnp.exp(draws), shape[dim] // shards_of).reshape((-1,) + (1,) * (len(shape) - dim - 1))

    factor_of = one(*cuts[0])
    for cut in cuts[1:]:
        factor_of = factor_of * one(*cut)
    return factor_of


def bell_draw(own_key, shape, deviation, bound, cuts=(), kind=jnp.bfloat16):
    entries = jax.random.normal(own_key, shape, jnp.float32) * deviation
    if len(cuts) > 0:
        entries = levels(own_key, shape, cuts, -0.22, 0.18) * entries
    return jnp.clip(entries, min=-bound, max=bound).astype(kind)


def noise_with(rng, extent, deviation, bound, cuts, heavy, kind=jnp.bfloat16):
    result = deviation * jax.random.normal(rng, extent, jnp.float32)
    if cuts:
        result = result * levels(rng, extent, cuts, -0.22, 0.18)
    return jnp.clip(raised(result, jax.random.fold_in(rng, 3), *heavy), -bound, bound).astype(kind)


def setup_inputs(seed: int = 0) -> dict:
    key_list = jax.random.split(jax.random.key(seed), 14)
    grid_fields = noise_with(key_list[0], (SAMPLES, GRID, C), 0.35, 2.09375, ((0, 16), (1, 16)), (1, 2, 16, 2.0))
    cotangent = bell_draw(key_list[1], (SAMPLES, NODES, D), 1.0, 6.0, ((0, 16), (1, 16)))
    encoder_source = with_ends(jax.random.randint(key_list[2], (NBLK, ECAP), 0, GRID), jax.random.fold_in(key_list[2], 1), 0, GRID - 1).astype(jnp.int32)
    encoder_target = with_ends(jax.random.randint(key_list[3], (NBLK, ECAP), 0, BLOCK), jax.random.fold_in(key_list[3], 1), 0, BLOCK - 1).astype(jnp.int32)
    encoder_count = draw_encoder_count(jax.random.fold_in(key_list[13], 71), 0)
    mesh_source = with_ends(jax.random.randint(key_list[5], (NBLK, PCAP), 0, NODES), jax.random.fold_in(key_list[5], 1), 0, NODES - 1).astype(jnp.int32)
    mesh_target = with_ends(jax.random.randint(key_list[6], (NBLK, PCAP), 0, BLOCK), jax.random.fold_in(key_list[6], 1), 0, BLOCK - 1).astype(jnp.int32)
    mesh_count = draw_mesh_count(jax.random.fold_in(key_list[13], 71), 0)
    w_encoder = bell_draw(key_list[8], (C, D), C ** -0.5, 0.5)
    w_query = bell_draw(key_list[9], (D, D), D ** -0.5, 0.1875)
    w_key = bell_draw(key_list[10], (D, D), D ** -0.5, 0.1875)
    w_value = bell_draw(key_list[11], (D, D), D ** -0.5, 0.1875)
    w_output = bell_draw(key_list[12], (D, D), D ** -0.5, 0.1875)
    return dict(grid_fields=grid_fields, cotangent=cotangent, encoder_source=encoder_source, encoder_target=encoder_target, encoder_count=encoder_count, mesh_source=mesh_source, mesh_target=mesh_target, mesh_count=mesh_count, w_encoder=w_encoder, w_query=w_query, w_key=w_key, w_value=w_value, w_output=w_output)


def widen(array):
    return array.astype(jnp.float32)

def reference(grid_fields, cotangent, encoder_source, encoder_target, encoder_count, mesh_source, mesh_target, mesh_count, w_encoder, w_query, w_key, w_value, w_output):
    samples, nodes, width = cotangent.shape
    channels = grid_fields.shape[2]
    blocks, enc_slots = encoder_source.shape
    mesh_slots = mesh_source.shape[1]
    block_base = jnp.arange(blocks, dtype=jnp.int32)[:, None] * BLOCK
    enc_alive = (jnp.arange(enc_slots, dtype=jnp.int32)[None, :] < encoder_count[:, None]).reshape(-1)
    enc_dest = (block_base + encoder_target).reshape(-1).astype(jnp.int32)
    enc_from = encoder_source.reshape(-1).astype(jnp.int32)
    mesh_alive = (jnp.arange(mesh_slots, dtype=jnp.int32)[None, :] < mesh_count[:, None]).reshape(-1)
    mesh_dest = (block_base + mesh_target).reshape(-1).astype(jnp.int32)
    mesh_from = mesh_source.reshape(-1).astype(jnp.int32)
    factor = 1.0 / math.sqrt(HD)

    def head_step(operands):
        query, key_rows, value, grad_mixed = operands
        query_edge = query[mesh_dest]
        key_edge = key_rows[mesh_from]
        value_edge = value[mesh_from]
        grad_edge = grad_mixed[mesh_dest]
        score = lax.optimization_barrier(jnp.sum(widen(query_edge) * widen(key_edge), axis=1)) * factor
        expo = jnp.where(mesh_alive, jnp.exp(score), 0.0)
        self_expo = jnp.exp(lax.optimization_barrier(jnp.sum(widen(query) * widen(key_rows), axis=1)) * factor)
        total = jax.ops.segment_sum(expo, mesh_dest, num_segments=nodes) + self_expo
        attn = expo / total[mesh_dest]
        attn_self = self_expo / total
        attn_round = attn.astype(jnp.bfloat16)
        self_round = attn_self.astype(jnp.bfloat16)
        attended = jax.ops.segment_sum(widen(attn_round)[:, None] * widen(value_edge), mesh_dest, num_segments=nodes)
        attended = (attended + widen(self_round)[:, None] * widen(value)).astype(jnp.bfloat16)
        dattn = lax.optimization_barrier(jnp.sum(widen(grad_edge) * widen(value_edge), axis=1))
        dattn_self = lax.optimization_barrier(jnp.sum(widen(grad_mixed) * widen(value), axis=1))
        mean_grad = jax.ops.segment_sum(attn * dattn, mesh_dest, num_segments=nodes) + attn_self * dattn_self
        grad_score = (attn * (dattn - mean_grad[mesh_dest]) * factor).astype(jnp.bfloat16)
        grad_self = (attn_self * (dattn_self - mean_grad) * factor).astype(jnp.bfloat16)
        grad_q = jax.ops.segment_sum(widen(grad_score)[:, None] * widen(key_edge), mesh_dest, num_segments=nodes)
        grad_q = (grad_q + widen(grad_self)[:, None] * widen(key_rows)).astype(jnp.bfloat16)
        grad_k = jax.ops.segment_sum(widen(grad_score)[:, None] * widen(query_edge), mesh_from, num_segments=nodes)
        grad_k = (grad_k + widen(grad_self)[:, None] * widen(query)).astype(jnp.bfloat16)
        grad_v = jax.ops.segment_sum(widen(attn_round)[:, None] * widen(grad_edge), mesh_from, num_segments=nodes)
        grad_v = (grad_v + widen(self_round)[:, None] * widen(grad_mixed)).astype(jnp.bfloat16)
        return (attended, grad_q, grad_k, grad_v)

    def split_heads(array):
        return array.reshape(nodes, HEADS, HD).transpose(1, 0, 2)

    def join_heads(array):
        return array.transpose(1, 0, 2).reshape(nodes, width)

    def per_sample(totals, inputs):
        sample_grid, sample_cot = inputs
        picked = jnp.where(enc_alive[:, None], widen(sample_grid[enc_from]), 0.0)
        encoded = jax.ops.segment_sum(picked, enc_dest, num_segments=nodes).astype(jnp.bfloat16)
        hidden = jnp.dot(encoded, w_encoder, preferred_element_type=jnp.float32).astype(jnp.bfloat16)
        query = jnp.dot(hidden, w_query, preferred_element_type=jnp.float32).astype(jnp.bfloat16)
        key_rows = jnp.dot(hidden, w_key, preferred_element_type=jnp.float32).astype(jnp.bfloat16)
        value = jnp.dot(hidden, w_value, preferred_element_type=jnp.float32).astype(jnp.bfloat16)
        grad_mixed = jnp.dot(sample_cot, w_output.T, preferred_element_type=jnp.float32).astype(jnp.bfloat16)
        results = lax.map(head_step, (split_heads(query), split_heads(key_rows), split_heads(value), split_heads(grad_mixed)))
        attended, grad_q, grad_k, grad_v = [join_heads(item) for item in results]
        grad_hidden = widen(sample_cot) + jnp.dot(grad_q, w_query.T, preferred_element_type=jnp.float32)
        grad_hidden = grad_hidden + jnp.dot(grad_k, w_key.T, preferred_element_type=jnp.float32)
        grad_hidden = (grad_hidden + jnp.dot(grad_v, w_value.T, preferred_element_type=jnp.float32)).astype(jnp.bfloat16)
        updated = (totals[0] + jnp.dot(hidden.T, grad_q, preferred_element_type=jnp.float32), totals[1] + jnp.dot(hidden.T, grad_k, preferred_element_type=jnp.float32), totals[2] + jnp.dot(hidden.T, grad_v, preferred_element_type=jnp.float32), totals[3] + jnp.dot(attended.T, sample_cot, preferred_element_type=jnp.float32), totals[4] + jnp.dot(encoded.T, grad_hidden, preferred_element_type=jnp.float32))
        return (updated, None)
    square = jnp.zeros((width, width), jnp.float32)
    start_totals = (square, square, square, square, jnp.zeros((channels, width), jnp.float32))
    totals, unused = lax.scan(per_sample, start_totals, (grid_fields, cotangent))
    norm = 1.0 / math.sqrt(samples * nodes)
    return (totals[0] * norm, totals[1] * norm, totals[2] * norm, totals[3] * norm, totals[4] * norm)
```

```python
import functools
import math

import jax
import jax.numpy as jnp
from jax import lax
from jax.experimental import pallas as pl
from jax.experimental.pallas import tpu as pltpu
from jax.sharding import PartitionSpec as P

BLOCK = 128
HD = 64
SLOT_CHUNK = 512
DEST_TILE = 256
ROW_CHUNK = 256
VMEM_LIMIT = 48 * 1024 * 1024


def dot_nn(left, right):
    return lax.dot_general(left, right, (((1,), (0,)), ((), ())), preferred_element_type=jnp.float32)


def dot_nt(left, right):
    return lax.dot_general(left, right, (((1,), (1,)), ((), ())), preferred_element_type=jnp.float32)


def dot_tn(left, right):
    return lax.dot_general(left, right, (((0,), (0,)), ((), ())), preferred_element_type=jnp.float32)


def encoder_kernel(
    count_ref, base_ref, source_ref, target_ref, grid_ref, w_output_ref, cot_ref, out_ref, pairs_ref
):
    block = pl.program_id(0)
    points = grid_ref.shape[0]
    slots = source_ref.shape[2]
    chunk = min(SLOT_CHUNK, slots)
    live = count_ref[block]
    base = base_ref[0]
    out_ref[0, BLOCK:, :] = dot_nt(w_output_ref[...], cot_ref[...]).astype(jnp.bfloat16)
    pairs_ref[...] = jnp.zeros_like(pairs_ref)

    def one_chunk(step, carry):
        first = pl.multiple_of(step * chunk, chunk)
        source = source_ref[0, :, pl.ds(first, chunk)] - base
        target = target_ref[0, :, pl.ds(first, chunk)]
        slot = first + lax.broadcasted_iota(jnp.int32, (1, chunk), 1)
        target = jnp.where(slot < live, target, -1)
        point_rows = lax.broadcasted_iota(jnp.int32, (points, chunk), 0)
        from_point = jnp.where(point_rows == source, 1.0, 0.0).astype(jnp.bfloat16)
        node_rows = lax.broadcasted_iota(jnp.int32, (BLOCK, chunk), 0)
        to_node = jnp.where(node_rows == target, 1.0, 0.0).astype(jnp.bfloat16)
        pairs_ref[...] += dot_nt(from_point, to_node)
        return carry

    lax.fori_loop(0, (live + chunk - 1) // chunk, one_chunk, 0)
    counts = pairs_ref[...].T.astype(jnp.bfloat16)
    out_ref[0, :BLOCK, :] = dot_nn(counts, grid_ref[...]).astype(jnp.bfloat16)


def encoder_partials(local_grid, source, target, count, base, w_output, local_cot):
    blocks, slots = source.shape
    points, channels = local_grid.shape
    node_rows, width = local_cot.shape
    head_rows = width // blocks
    return pl.pallas_call(
        encoder_kernel,
        grid_spec=pltpu.PrefetchScalarGridSpec(
            num_scalar_prefetch=2,
            grid=(blocks,),
            in_specs=[
                pl.BlockSpec((1, 1, slots), lambda b, *_: (b, 0, 0)),
                pl.BlockSpec((1, 1, slots), lambda b, *_: (b, 0, 0)),
                pl.BlockSpec((points, channels), lambda b, *_: (0, 0)),
                pl.BlockSpec((head_rows, width), lambda b, *_: (b, 0)),
                pl.BlockSpec((node_rows, width), lambda b, *_: (0, 0)),
            ],
            out_specs=pl.BlockSpec((1, BLOCK + head_rows, channels), lambda b, *_: (b, 0, 0)),
            scratch_shapes=[pltpu.VMEM((points, BLOCK), jnp.float32)],
        ),
        out_shape=jax.ShapeDtypeStruct((blocks, BLOCK + head_rows, channels), jnp.bfloat16),
        compiler_params=pltpu.CompilerParams(vmem_limit_bytes=VMEM_LIMIT),
        cost_estimate=pl.CostEstimate(
            flops=2 * blocks * slots * points * BLOCK, bytes_accessed=2 * points * channels, transcendentals=0
        ),
    )(
        count,
        base,
        source.reshape(blocks, 1, slots),
        target.reshape(blocks, 1, slots),
        local_grid,
        w_output,
        local_cot,
    )


def edges_kernel(count_ref, source_ref, target_ref, out_ref):
    block = pl.program_id(0)
    nodes = out_ref.shape[0]
    slots = source_ref.shape[2]
    slot = lax.broadcasted_iota(jnp.int32, (1, slots), 1)
    target = jnp.where(slot < count_ref[block], target_ref[0], -1)
    node_rows = lax.broadcasted_iota(jnp.int32, (BLOCK, slots), 0)
    to_node = jnp.where(node_rows == target, 1.0, 0.0).astype(jnp.bfloat16)
    from_rows = lax.broadcasted_iota(jnp.int32, (nodes, slots), 0)
    from_node = jnp.where(from_rows == source_ref[0], 1.0, 0.0).astype(jnp.bfloat16)
    out_ref[...] = dot_nt(from_node, to_node).astype(jnp.bfloat16)
    start = pl.multiple_of(block * BLOCK, BLOCK)
    diagonal = lax.broadcasted_iota(jnp.int32, (BLOCK, BLOCK), 0) == lax.broadcasted_iota(
        jnp.int32, (BLOCK, BLOCK), 1
    )
    own = out_ref[pl.ds(start, BLOCK), :].astype(jnp.float32)
    out_ref[pl.ds(start, BLOCK), :] = (own + jnp.where(diagonal, 1.0, 0.0)).astype(jnp.bfloat16)


def edge_counts(source, target, count, nodes):
    blocks, slots = source.shape
    return pl.pallas_call(
        edges_kernel,
        grid_spec=pltpu.PrefetchScalarGridSpec(
            num_scalar_prefetch=1,
            grid=(blocks,),
            in_specs=[
                pl.BlockSpec((1, 1, slots), lambda b, *_: (b, 0, 0)),
                pl.BlockSpec((1, 1, slots), lambda b, *_: (b, 0, 0)),
            ],
            out_specs=pl.BlockSpec((nodes, BLOCK), lambda b, *_: (0, b)),
        ),
        out_shape=jax.ShapeDtypeStruct((nodes, nodes), jnp.bfloat16),
        compiler_params=pltpu.CompilerParams(vmem_limit_bytes=VMEM_LIMIT),
        cost_estimate=pl.CostEstimate(
            flops=2 * nodes * blocks * slots * BLOCK * 2, bytes_accessed=2 * nodes * nodes, transcendentals=0
        ),
    )(count, source.reshape(blocks, 1, slots), target.reshape(blocks, 1, slots))


def attention_kernel(
    index_ref,
    encoded_ref,
    w_encoder_ref,
    w_head_ref,
    received_ref,
    pairs_ref,
    left_ref,
    grads_ref,
    hidden_s,
    query_s,
    key_s,
    value_s,
    grad_s,
    queryt_s,
    keyt_s,
    valuet_s,
    gradt_s,
    encodedt_s,
    expo_s,
    dattn_s,
    attn_s,
    dscore_s,
    grad_qt_s,
    grad_k_s,
    grad_v_s,
):
    step = pl.program_id(0)
    blocks, block_rows, channels = encoded_ref.shape
    nodes = blocks * block_rows
    width = w_encoder_ref.shape[1]
    factor = 1.0 / math.sqrt(HD)

    @pl.when(step == 0)
    def _():
        def one_rows(index, carry):
            rows = pl.ds(pl.multiple_of(index * ROW_CHUNK, ROW_CHUNK), ROW_CHUNK)
            pair = ROW_CHUNK // block_rows
            encoded = encoded_ref[pl.ds(index * pair, pair)].reshape(ROW_CHUNK, channels)
            hidden = dot_nn(encoded, w_encoder_ref[...]).astype(jnp.bfloat16)
            hidden_s[rows, :] = hidden
            mixed = dot_nn(hidden, w_head_ref[...])
            query_s[rows, :] = mixed[:, :HD].astype(jnp.bfloat16)
            key_s[rows, :] = mixed[:, HD : 2 * HD].astype(jnp.bfloat16)
            value_s[rows, :] = mixed[:, 2 * HD :].astype(jnp.bfloat16)
            flipped = mixed.T
            queryt_s[:, rows] = flipped[:HD, :].astype(jnp.bfloat16)
            keyt_s[:, rows] = flipped[HD : 2 * HD, :].astype(jnp.bfloat16)
            valuet_s[:, rows] = flipped[2 * HD :, :].astype(jnp.bfloat16)
            return carry

        lax.fori_loop(0, nodes // ROW_CHUNK, one_rows, 0)
        for block in range(blocks):
            rows = slice(block * block_rows, (block + 1) * block_rows)
            gradt = received_ref[block, block_rows:, :]
            gradt_s[:, rows] = gradt
            grad_s[rows, :] = gradt.astype(jnp.float32).T.astype(jnp.bfloat16)
            encodedt_s[:, rows] = encoded_ref[block].astype(jnp.float32).T
        grad_k_s[...] = jnp.zeros_like(grad_k_s)
        grad_v_s[...] = jnp.zeros_like(grad_v_s)

    dest = pl.ds(pl.multiple_of(step * DEST_TILE, DEST_TILE), DEST_TILE)
    queryt = queryt_s[:, dest] * jnp.bfloat16(factor)
    gradt = gradt_s[:, dest]
    total = jnp.zeros((1, DEST_TILE), jnp.float32)
    weighted = jnp.zeros((1, DEST_TILE), jnp.float32)
    for index in range(nodes // ROW_CHUNK):
        rows = slice(index * ROW_CHUNK, (index + 1) * ROW_CHUNK)
        score = dot_nn(key_s[rows, :], queryt)
        times = pairs_ref[rows, :].astype(jnp.float32)
        expo = jnp.where(times > 0.0, jnp.exp(score), 0.0) * times
        dattn = dot_nn(value_s[rows, :], gradt)
        expo_s[rows, :] = expo
        dattn_s[rows, :] = dattn
        total += jnp.sum(expo, axis=0, keepdims=True)
        weighted += jnp.sum(expo * dattn, axis=0, keepdims=True)
    inverse = 1.0 / total
    mean_grad = weighted * inverse
    for index in range(nodes // ROW_CHUNK):
        rows = slice(index * ROW_CHUNK, (index + 1) * ROW_CHUNK)
        attn = expo_s[rows, :] * inverse
        attn_s[rows, :] = attn.astype(jnp.bfloat16)
        dscore_s[rows, :] = (attn * (dattn_s[rows, :] - mean_grad) * factor).astype(jnp.bfloat16)
    left_ref[:HD, :] = dot_nn(valuet_s[...], attn_s[...]).astype(jnp.bfloat16)
    own = left_ref.shape[0] - HD
    left_ref[HD:, :] = encodedt_s[
        pl.ds(pl.multiple_of(index_ref[0] * own, own), own), dest
    ].astype(jnp.bfloat16)
    grad_qt_s[:, dest] = dot_nn(keyt_s[...], dscore_s[...]).astype(jnp.bfloat16)
    grad_k_s[...] += dot_nn(dscore_s[...], query_s[dest, :])
    grad_v_s[...] += dot_nn(attn_s[...], grad_s[dest, :])

    @pl.when(step == pl.num_programs(0) - 1)
    def _():
        gradst = jnp.concatenate(
            [grad_qt_s[...], grad_k_s[...].T.astype(jnp.bfloat16), grad_v_s[...].T.astype(jnp.bfloat16)],
            axis=0,
        )
        parts = grads_ref.shape[0]
        piece = width // parts
        weights = dot_nn(gradst, hidden_s[...]).T.astype(jnp.bfloat16)
        grads_ref[:, :piece, :] = weights.reshape(parts, piece, 3 * HD)
        terms = dot_nn(gradst, encoded_ref[...].reshape(nodes, channels)).T.astype(jnp.bfloat16)
        own_rows = channels // parts
        for part in range(parts):
            grads_ref[part, piece:, :] = terms[part * own_rows : (part + 1) * own_rows, :]


def attention(index, encoded, w_encoder, w_head, received, pairs, parts):
    blocks, block_rows, channels = encoded.shape
    nodes = blocks * block_rows
    width = w_encoder.shape[1]
    whole = lambda *shape: pl.BlockSpec(shape, lambda j, *_: (0,) * len(shape))
    half, full = jnp.bfloat16, jnp.float32
    rows = HD + channels // parts
    return pl.pallas_call(
        attention_kernel,
        grid_spec=pltpu.PrefetchScalarGridSpec(
            num_scalar_prefetch=1,
            grid=(nodes // DEST_TILE,),
            in_specs=[
                whole(blocks, block_rows, channels),
                whole(channels, width),
                whole(width, 3 * HD),
                whole(*received.shape),
                pl.BlockSpec((nodes, DEST_TILE), lambda j, *_: (0, j)),
            ],
            out_specs=[
                pl.BlockSpec((rows, DEST_TILE), lambda j, *_: (0, j)),
                whole(parts, rows, 3 * HD),
            ],
            scratch_shapes=[
                pltpu.VMEM((nodes, width), half),
                pltpu.VMEM((nodes, HD), half),
                pltpu.VMEM((nodes, HD), half),
                pltpu.VMEM((nodes, HD), half),
                pltpu.VMEM((nodes, HD), half),
                pltpu.VMEM((HD, nodes), half),
                pltpu.VMEM((HD, nodes), half),
                pltpu.VMEM((HD, nodes), half),
                pltpu.VMEM((HD, nodes), half),
                pltpu.VMEM((channels, nodes), full),
                pltpu.VMEM((nodes, DEST_TILE), full),
                pltpu.VMEM((nodes, DEST_TILE), full),
                pltpu.VMEM((nodes, DEST_TILE), half),
                pltpu.VMEM((nodes, DEST_TILE), half),
                pltpu.VMEM((HD, nodes), half),
                pltpu.VMEM((nodes, HD), full),
                pltpu.VMEM((nodes, HD), full),
            ],
        ),
        out_shape=[
            jax.ShapeDtypeStruct((rows, nodes), half),
            jax.ShapeDtypeStruct((parts, rows, 3 * HD), half),
        ],
        compiler_params=pltpu.CompilerParams(vmem_limit_bytes=VMEM_LIMIT),
        cost_estimate=pl.CostEstimate(
            flops=12 * nodes * nodes * HD, bytes_accessed=2 * nodes * nodes, transcendentals=nodes * nodes
        ),
    )(index, encoded, w_encoder, w_head, received, pairs)


def meet_kernel(left_ref, cot_ref, grads_ref, out_ref):
    met = dot_nn(left_ref[...], cot_ref[...]).astype(jnp.bfloat16)
    parts = grads_ref.shape[0]
    piece = met.shape[1] // parts
    for part in range(parts):
        out_ref[part] = jnp.concatenate(
            [grads_ref[part], met[:, part * piece : (part + 1) * piece]], axis=1
        )


def meet(left, all_cot, grads):
    rows, nodes = left.shape
    width = all_cot.shape[1]
    parts, _, columns = grads.shape
    tiles = 4
    piece = width // parts
    return pl.pallas_call(
        meet_kernel,
        grid=(tiles,),
        in_specs=[
            pl.BlockSpec((rows, nodes), lambda j: (0, 0)),
            pl.BlockSpec((nodes, width // tiles), lambda j: (0, j)),
            pl.BlockSpec((parts // tiles, rows, columns), lambda j: (j, 0, 0)),
        ],
        out_specs=pl.BlockSpec((parts // tiles, rows, columns + piece), lambda j: (j, 0, 0)),
        out_shape=jax.ShapeDtypeStruct((parts, rows, columns + piece), jnp.bfloat16),
        compiler_params=pltpu.CompilerParams(vmem_limit_bytes=VMEM_LIMIT),
        cost_estimate=pl.CostEstimate(
            flops=2 * rows * nodes * width, bytes_accessed=2 * nodes * width, transcendentals=0
        ),
    )(left, all_cot, grads)


def finish_kernel(
    norm, sums_ref, w_query_ref, w_key_ref, w_value_ref, query_ref, key_ref, value_ref, output_ref, encoder_ref
):
    parts, rows, _ = sums_ref.shape
    outs = (query_ref, key_ref, value_ref, output_ref)
    for part in range(parts):
        piece = sums_ref[part].astype(jnp.float32) * norm
        columns = slice(part * HD, (part + 1) * HD)
        for place, out in enumerate(outs):
            out[:, columns] = piece[:HD, place * HD : (place + 1) * HD]
        encoder_ref[:, columns] = piece[HD:, 3 * HD :]
    encoder = encoder_ref[...]
    for place, weight in enumerate((w_query_ref, w_key_ref, w_value_ref)):
        terms = jnp.concatenate(
            [sums_ref[part, HD:, place * HD : (place + 1) * HD] for part in range(parts)], axis=1
        )
        encoder += dot_nt(terms, weight[...]) * norm
    encoder_ref[...] = encoder


def finish(sums, w_query, w_key, w_value, norm):
    parts, rows, _ = sums.shape
    width = w_query.shape[0]
    full = jnp.float32
    return pl.pallas_call(
        functools.partial(finish_kernel, norm),
        out_shape=[jax.ShapeDtypeStruct((HD, width), full)] * 4
        + [jax.ShapeDtypeStruct((rows - HD, width), full)],
        compiler_params=pltpu.CompilerParams(vmem_limit_bytes=VMEM_LIMIT),
    )(sums, w_query, w_key, w_value)


def spread(array, axis):
    size = lax.axis_size(axis)
    copies = jnp.broadcast_to(array[None], (size,) + array.shape)
    return lax.all_to_all(copies, axis, split_axis=0, concat_axis=0, tiled=True)


def per_device(
    grid_fields,
    cotangent,
    encoder_source,
    encoder_target,
    encoder_count,
    mesh_source,
    mesh_target,
    mesh_count,
    w_encoder,
    w_query,
    w_key,
    w_value,
    w_output,
):
    model_size = lax.axis_size("mp")
    data_size = lax.axis_size("dp")
    model_index = lax.axis_index("mp")
    local_grid = grid_fields[0]
    local_cot = cotangent[0]
    points, channels = local_grid.shape
    node_rows, width = local_cot.shape
    nodes = node_rows * model_size
    half = jnp.bfloat16

    other = lax.ppermute(local_cot, "mp", [(i, i ^ 1) for i in range(model_size)])
    odd = model_index % 2 == 1
    both = jnp.concatenate([jnp.where(odd, other, local_cot), jnp.where(odd, local_cot, other)], axis=0)
    lanes = [list(range(first, model_size, 2)) for first in range(2)]
    all_cot = lax.all_gather(both, "mp", axis=0, tiled=True, axis_index_groups=lanes)

    partials = encoder_partials(
        local_grid,
        encoder_source,
        encoder_target,
        encoder_count,
        (model_index * points).reshape(1).astype(jnp.int32),
        w_output,
        local_cot,
    )
    received = lax.all_to_all(partials, "mp", split_axis=0, concat_axis=0, tiled=True)
    own_encoded = jnp.sum(received[:, :node_rows].astype(jnp.float32), axis=0).astype(half)
    encoded = spread(own_encoded, "mp")

    pairs = edge_counts(mesh_source, mesh_target, mesh_count, nodes)
    first = model_index * HD
    w_head = jnp.concatenate(
        [lax.dynamic_slice_in_dim(item, first, HD, 1) for item in (w_query, w_key, w_value)], axis=1
    )
    left, grads = attention(
        model_index.reshape(1).astype(jnp.int32), encoded, w_encoder, w_head, received, pairs, data_size
    )
    shares = meet(left, all_cot, grads)

    shares = lax.all_to_all(shares, "dp", split_axis=0, concat_axis=0, tiled=True)
    share = jnp.sum(shares.astype(jnp.float32), axis=0).astype(half)
    across = [
        (data * model_size + model, model * model_size + data)
        for data in range(data_size)
        for model in range(model_size)
    ]
    swapped = lax.ppermute(share, ("dp", "mp"), across)
    column = lax.broadcasted_iota(jnp.int32, share.shape, 1)
    share = jnp.where(column < 3 * HD, swapped, share)
    sums = spread(share, "dp")
    norm = 1.0 / math.sqrt(data_size * nodes)
    return tuple(finish(sums, w_query, w_key, w_value, norm))


def solution(mesh):
    in_specs = (
        P("dp", "mp", None),
        P("dp", "mp", None),
        P(),
        P(),
        P(),
        P(),
        P(),
        P(),
        P(),
        P(),
        P(),
        P(),
        P(),
    )
    out_specs = (P("mp", None), P("mp", None), P("mp", None), P("mp", None), P("mp", None))
    return jax.shard_map(
        per_device, mesh=mesh, in_specs=in_specs, out_specs=out_specs, check_vma=False
    )
```

```python
import functools
import math

import jax
import jax.numpy as jnp
from jax import lax
from jax.experimental import pallas as pl
from jax.experimental.pallas import tpu as pltpu
from jax.sharding import PartitionSpec as P

BLOCK = 128
HD = 64
LOW = 256
FIRST_SLOTS = 1024
EDGE_BLOCKS = 4
DEST_TILE = 256
ROW_CHUNK = 256
MEET_TILES = 4
WIDE = 60 * 1024 * 1024
SMALL = 12 * 1024 * 1024
ROOM = 24 * 1024 * 1024
half = jnp.bfloat16
full = jnp.float32


def dot_nn(left, right):
    return lax.dot_general(left, right, (((1,), (0,)), ((), ())), preferred_element_type=full)


def dot_nt(left, right):
    return lax.dot_general(left, right, (((1,), (1,)), ((), ())), preferred_element_type=full)


def whole(*shape):
    return pl.BlockSpec(shape, lambda *_: (0,) * len(shape))


def one_hot(rows, index):
    place = lax.broadcasted_iota(jnp.int32, (rows, index.shape[1]), 0)
    return jnp.where(place == index, 1.0, 0.0).astype(half)


def encoder_kernel(
    count_ref, base_ref, source_ref, target_ref, grid_ref, w_output_ref, cot_ref, out_ref, pairs_ref, w_s, sem
):
    blocks = source_ref.shape[0]
    points = grid_ref.shape[0]
    highs = points // LOW
    base = base_ref[0]
    fetch = pltpu.make_async_copy(w_output_ref, w_s, sem)
    fetch.start()

    def pair_counts(block, first):
        source = source_ref[block : block + 1, pl.ds(first, FIRST_SLOTS)] - base
        target = target_ref[block : block + 1, pl.ds(first, FIRST_SLOTS)]
        slot = first + lax.broadcasted_iota(jnp.int32, (1, FIRST_SLOTS), 1)
        used = (slot < count_ref[block]) & (source >= 0) & (source < points)
        column = jnp.where(used, lax.shift_right_logical(source, 8) * BLOCK + target, -1)
        return dot_nt(one_hot(highs * BLOCK, column), one_hot(LOW, source & (LOW - 1)))

    for block in range(blocks):
        pairs_ref[block] = pair_counts(block, 0)
    for block in range(blocks):

        def more(step, carry, block=block):
            pairs_ref[block] += pair_counts(block, pl.multiple_of(step * FIRST_SLOTS, FIRST_SLOTS))
            return carry

        lax.fori_loop(1, (count_ref[block] + FIRST_SLOTS - 1) // FIRST_SLOTS, more, 0)
    for block in range(blocks):
        counts = pairs_ref[block].astype(half)
        sums = dot_nn(counts[:BLOCK], grid_ref[:LOW])
        for high in range(1, highs):
            sums += dot_nn(
                counts[high * BLOCK : (high + 1) * BLOCK], grid_ref[high * LOW : (high + 1) * LOW]
            )
        out_ref[block, :BLOCK, :] = sums.astype(half)
    fetch.wait()
    mixed = dot_nt(w_s[...], cot_ref[...]).astype(half)
    heads = mixed.shape[0] // blocks
    for block in range(blocks):
        out_ref[block, BLOCK:, :] = mixed[block * heads : (block + 1) * heads]


def encoder_partials(local_grid, source, target, count, base, w_output, local_cot):
    blocks, slots = source.shape
    points, channels = local_grid.shape
    node_rows, width = local_cot.shape
    head_rows = width // blocks
    return pl.pallas_call(
        encoder_kernel,
        grid_spec=pltpu.PrefetchScalarGridSpec(
            num_scalar_prefetch=2,
            grid=(1,),
            in_specs=[
                whole(blocks, slots),
                whole(blocks, slots),
                whole(points, channels),
                pl.BlockSpec(memory_space=pl.ANY),
                whole(node_rows, width),
            ],
            out_specs=whole(blocks, BLOCK + head_rows, channels),
            scratch_shapes=[
                pltpu.VMEM((blocks, points // LOW * BLOCK, LOW), full),
                pltpu.VMEM((width, width), half),
                pltpu.SemaphoreType.DMA,
            ],
        ),
        out_shape=jax.ShapeDtypeStruct((blocks, BLOCK + head_rows, channels), half),
        compiler_params=pltpu.CompilerParams(vmem_limit_bytes=WIDE),
        cost_estimate=pl.CostEstimate(
            flops=2 * blocks * slots * points * BLOCK, bytes_accessed=2 * points * channels, transcendentals=0
        ),
    )(count, base, source, target, local_grid, w_output, local_cot)


def collect_kernel(odd_ref, received_ref, own_ref, other_ref, copies_ref, both_ref):
    parts, rows, _ = copies_ref.shape
    total = received_ref[0, :rows, :].astype(full)
    for part in range(1, parts):
        total += received_ref[part, :rows, :].astype(full)
    total = total.astype(half)
    for part in range(parts):
        copies_ref[part] = total
    own, other = own_ref[...], other_ref[...]
    odd = odd_ref[0] == 1

    @pl.when(odd)
    def _():
        both_ref[:rows, :] = other
        both_ref[rows:, :] = own

    @pl.when(jnp.logical_not(odd))
    def _():
        both_ref[:rows, :] = own
        both_ref[rows:, :] = other


def collect(odd, received, own, other):
    parts, _, channels = received.shape
    rows, width = own.shape
    return pl.pallas_call(
        collect_kernel,
        grid_spec=pltpu.PrefetchScalarGridSpec(
            num_scalar_prefetch=1,
            grid=(1,),
            in_specs=[whole(*received.shape), whole(rows, width), whole(rows, width)],
            out_specs=[whole(parts, rows, channels), whole(2 * rows, width)],
        ),
        out_shape=[
            jax.ShapeDtypeStruct((parts, rows, channels), half),
            jax.ShapeDtypeStruct((2 * rows, width), half),
        ],
        compiler_params=pltpu.CompilerParams(vmem_limit_bytes=SMALL),
    )(odd, received, own, other)


def edges_kernel(count_ref, source_ref, target_ref, out_ref):
    slots = source_ref.shape[1]
    nodes, columns_here = out_ref.shape
    blocks = columns_here // BLOCK
    highs = nodes // LOW
    first_block = pl.program_id(0) * blocks
    slot = lax.broadcasted_iota(jnp.int32, (1, slots), 1)
    rows = lax.broadcasted_iota(jnp.int32, (LOW, BLOCK), 0)
    columns = lax.broadcasted_iota(jnp.int32, (LOW, BLOCK), 1)
    for block in range(blocks):
        source = source_ref[pl.ds(first_block + block, 1), :]
        target = target_ref[pl.ds(first_block + block, 1), :]
        used = slot < count_ref[first_block + block]
        column = jnp.where(used, lax.shift_right_logical(source, 8) * BLOCK + target, -1)
        counts = dot_nt(one_hot(LOW, source & (LOW - 1)), one_hot(highs * BLOCK, column))
        for high in range(highs):
            own = jnp.where(high * LOW + rows == (first_block + block) * BLOCK + columns, 1.0, 0.0)
            out_ref[high * LOW : (high + 1) * LOW, block * BLOCK : (block + 1) * BLOCK] = (
                counts[:, high * BLOCK : (high + 1) * BLOCK] + own
            ).astype(half)


def edge_counts(source, target, count, nodes):
    blocks, slots = source.shape
    some = EDGE_BLOCKS
    return pl.pallas_call(
        edges_kernel,
        grid_spec=pltpu.PrefetchScalarGridSpec(
            num_scalar_prefetch=1,
            grid=(blocks // some,),
            in_specs=[
                whole(blocks, slots),
                whole(blocks, slots),
            ],
            out_specs=pl.BlockSpec((nodes, some * BLOCK), lambda b, *_: (0, b)),
        ),
        out_shape=jax.ShapeDtypeStruct((nodes, nodes), half),
        compiler_params=pltpu.CompilerParams(vmem_limit_bytes=WIDE),
        cost_estimate=pl.CostEstimate(
            flops=2 * nodes * blocks * slots * BLOCK * 2, bytes_accessed=2 * nodes * nodes, transcendentals=0
        ),
    )(count, source, target)


def attention_kernel(
    index_ref,
    encoded_ref,
    w_encoder_ref,
    w_query_ref,
    w_key_ref,
    w_value_ref,
    received_ref,
    pairs_ref,
    left_ref,
    grads_ref,
    hidden_s,
    query_s,
    key_s,
    value_s,
    queryt_s,
    keyt_s,
    valuet_s,
    gradt_s,
    expo_s,
    dattn_s,
    grad_qt_s,
    grad_kv_s,
):
    step = pl.program_id(0)
    blocks, block_rows, channels = encoded_ref.shape
    nodes = blocks * block_rows
    width = w_encoder_ref.shape[1]
    factor = 1.0 / math.sqrt(HD)

    @pl.when(step == 0)
    def _():
        encoded = encoded_ref[...].reshape(nodes, channels)
        odd = index_ref[0] % 2 == 1
        w_head = jnp.concatenate(
            [jnp.where(odd, ref[:, HD:], ref[:, :HD]) for ref in (w_query_ref, w_key_ref, w_value_ref)], axis=1
        )
        for index in range(nodes // ROW_CHUNK):
            rows = slice(index * ROW_CHUNK, (index + 1) * ROW_CHUNK)
            hidden = dot_nn(encoded[rows], w_encoder_ref[...]).astype(half)
            hidden_s[rows, :] = hidden
            mixed = dot_nn(hidden, w_head)
            query_s[rows, :] = mixed[:, :HD].astype(half)
            key_s[rows, :] = mixed[:, HD : 2 * HD].astype(half)
            value_s[rows, :] = mixed[:, 2 * HD :].astype(half)
            flipped = mixed.T
            queryt_s[:, rows] = (flipped[:HD, :] * factor).astype(half)
            keyt_s[:, rows] = (flipped[HD : 2 * HD, :] * factor).astype(half)
            valuet_s[:, rows] = flipped[2 * HD :, :].astype(half)
        for block in range(blocks):
            gradt_s[:, block * block_rows : (block + 1) * block_rows] = received_ref[block, block_rows:, :]
        grad_kv_s[...] = jnp.zeros_like(grad_kv_s)

    dest = pl.ds(pl.multiple_of(step * DEST_TILE, DEST_TILE), DEST_TILE)
    queryt, gradt = queryt_s[:, dest], gradt_s[:, dest]
    query, grad = query_s[dest, :], gradt.astype(full).T.astype(half)
    none = jnp.zeros((DEST_TILE, HD), half)
    sides = jnp.concatenate([jnp.concatenate([query, none], axis=1), jnp.concatenate([none, grad], axis=1)], axis=0)
    total = jnp.zeros((1, DEST_TILE), full)
    weighted = jnp.zeros((1, DEST_TILE), full)
    for index in range(nodes // ROW_CHUNK):
        rows = slice(index * ROW_CHUNK, (index + 1) * ROW_CHUNK)
        score = dot_nn(key_s[rows, :], queryt)
        times = pairs_ref[rows, :].astype(full)
        expo = jnp.where(times > 0.0, jnp.exp(score), 0.0) * times
        dattn = dot_nn(value_s[rows, :], gradt)
        expo_s[rows, :] = expo
        dattn_s[rows, :] = dattn
        total += jnp.sum(expo, axis=0, keepdims=True)
        weighted += jnp.sum(expo * dattn, axis=0, keepdims=True)
    inverse = 1.0 / total
    mean_grad = weighted * inverse
    attended = jnp.zeros((HD, DEST_TILE), full)
    grad_qt = jnp.zeros((HD, DEST_TILE), full)
    for index in range(nodes // ROW_CHUNK):
        rows = slice(index * ROW_CHUNK, (index + 1) * ROW_CHUNK)
        attn = expo_s[rows, :] * inverse
        attn_round = attn.astype(half)
        dscore = (attn * (dattn_s[rows, :] - mean_grad)).astype(half)
        attended += dot_nn(valuet_s[:, rows], attn_round)
        grad_qt += dot_nn(keyt_s[:, rows], dscore)
        grad_kv_s[rows, :] += dot_nn(jnp.concatenate([dscore, attn_round], axis=1), sides)
    own = channels // grads_ref.shape[0]
    spare = left_ref.shape[0] - HD
    channel = lax.broadcasted_iota(jnp.int32, (spare, channels), 1)
    row = lax.broadcasted_iota(jnp.int32, (spare, channels), 0)
    pick = (channel == index_ref[0] * own + row) & (row < own)
    pair = DEST_TILE // block_rows
    here = encoded_ref[pl.ds(step * pair, pair)].reshape(DEST_TILE, channels)
    picked = dot_nt(jnp.where(pick, 1.0, 0.0).astype(half), here)
    left_ref[...] = jnp.concatenate([attended, picked], axis=0).astype(half)
    grad_qt_s[:, dest] = grad_qt.astype(half)

    @pl.when(step == pl.num_programs(0) - 1)
    def _():
        grad_kvt = grad_kv_s[...].T
        gradst = jnp.concatenate(
            [grad_qt_s[...], (grad_kvt[:HD] * factor).astype(half), grad_kvt[HD:].astype(half)], axis=0
        )
        parts = grads_ref.shape[0]
        weights = dot_nn(gradst, hidden_s[...]).T
        terms = dot_nn(gradst, encoded_ref[...].reshape(nodes, channels)).T
        piece = width // parts
        for part in range(parts):
            weight = weights[part * piece : (part + 1) * piece, :]
            term = terms[part * own : (part + 1) * own, :]
            grads_ref[(part - index_ref[0] + parts) % parts] = jnp.concatenate(
                [
                    weight[:, : 2 * HD],
                    term[:, : 2 * HD],
                    jnp.concatenate([weight[: piece // 2, 2 * HD :], weight[piece // 2 :, 2 * HD :]], axis=1),
                    jnp.concatenate([term[:, 2 * HD :], jnp.zeros((own, HD), full)], axis=1),
                ],
                axis=0,
            ).astype(half)


def attention(index, encoded, w_encoder, w_query, w_key, w_value, received, pairs, parts):
    blocks, block_rows, channels = encoded.shape
    nodes = blocks * block_rows
    width = w_encoder.shape[1]
    own = channels // parts
    left_rows = HD + 2 * own
    rows = HD + own + HD // 2 + own
    return pl.pallas_call(
        attention_kernel,
        grid_spec=pltpu.PrefetchScalarGridSpec(
            num_scalar_prefetch=1,
            grid=(nodes // DEST_TILE,),
            in_specs=[
                whole(blocks, block_rows, channels),
                whole(channels, width),
                pl.BlockSpec((width, 2 * HD), lambda j, m: (0, m[0] // 2)),
                pl.BlockSpec((width, 2 * HD), lambda j, m: (0, m[0] // 2)),
                pl.BlockSpec((width, 2 * HD), lambda j, m: (0, m[0] // 2)),
                whole(*received.shape),
                pl.BlockSpec((nodes, DEST_TILE), lambda j, *_: (0, j)),
            ],
            out_specs=[
                pl.BlockSpec((left_rows, DEST_TILE), lambda j, *_: (0, j)),
                whole(parts, rows, 2 * HD),
            ],
            scratch_shapes=[
                pltpu.VMEM((nodes, width), half),
                pltpu.VMEM((nodes, HD), half),
                pltpu.VMEM((nodes, HD), half),
                pltpu.VMEM((nodes, HD), half),
                pltpu.VMEM((HD, nodes), half),
                pltpu.VMEM((HD, nodes), half),
                pltpu.VMEM((HD, nodes), half),
                pltpu.VMEM((HD, nodes), half),
                pltpu.VMEM((nodes, DEST_TILE), full),
                pltpu.VMEM((nodes, DEST_TILE), full),
                pltpu.VMEM((HD, nodes), half),
                pltpu.VMEM((nodes, 2 * HD), full),
            ],
        ),
        out_shape=[
            jax.ShapeDtypeStruct((left_rows, nodes), half),
            jax.ShapeDtypeStruct((parts, rows, 2 * HD), half),
        ],
        compiler_params=pltpu.CompilerParams(vmem_limit_bytes=WIDE),
        cost_estimate=pl.CostEstimate(
            flops=12 * nodes * nodes * HD, bytes_accessed=2 * nodes * nodes, transcendentals=nodes * nodes
        ),
    )(index, encoded, w_encoder, w_query, w_key, w_value, received, pairs)


def meet_kernel(own, left_ref, cot_ref, out_ref, cot_s, sems):
    nodes, width = cot_ref.shape
    some = nodes // MEET_TILES
    copies = []
    for tile in range(MEET_TILES):
        rows = pl.ds(tile * some, some)
        copies.append(pltpu.make_async_copy(cot_ref.at[rows, :], cot_s.at[rows, :], sems.at[tile]))
        copies[-1].start()
    met = jnp.zeros((left_ref.shape[0], width), full)
    for tile in range(MEET_TILES):
        copies[tile].wait()
        rows = slice(tile * some, (tile + 1) * some)
        met += dot_nn(left_ref[:, rows], cot_s[rows, :])
    parts, rows, columns = out_ref.shape
    piece = width // parts
    spare = rows - HD // 2 - own
    for part in range(parts):
        mine = met[:, part * piece : (part + 1) * piece]
        out_ref[part] = jnp.concatenate(
            [
                jnp.concatenate([mine[: HD // 2], mine[HD // 2 : HD]], axis=1),
                jnp.concatenate([jnp.zeros((own, piece), full), mine[HD : HD + own]], axis=1),
                jnp.zeros((spare, columns), full),
            ],
            axis=0,
        ).astype(half)


def meet(left, all_cot, parts, own):
    rows, nodes = left.shape
    width = all_cot.shape[1]
    out_rows = HD // 2 + 2 * own
    return pl.pallas_call(
        functools.partial(meet_kernel, own),
        grid=(1,),
        in_specs=[whole(rows, nodes), pl.BlockSpec(memory_space=pl.ANY)],
        out_specs=whole(parts, out_rows, 2 * HD),
        out_shape=jax.ShapeDtypeStruct((parts, out_rows, 2 * HD), half),
        scratch_shapes=[pltpu.VMEM((nodes, width), half), pltpu.SemaphoreType.DMA((MEET_TILES,))],
        compiler_params=pltpu.CompilerParams(vmem_limit_bytes=WIDE),
        cost_estimate=pl.CostEstimate(
            flops=2 * rows * nodes * width, bytes_accessed=2 * nodes * width, transcendentals=0
        ),
    )(left, all_cot)


def add_parts(ref):
    total = ref[0].astype(full)
    for part in range(1, ref.shape[0]):
        total += ref[part].astype(full)
    return total


def join_kernel(own, met_ref, swapped_ref, out_ref):
    met = add_parts(met_ref)
    swapped = swapped_ref[...].astype(full)
    half_rows = HD // 2
    last = swapped.shape[0] - own
    joined = jnp.concatenate(
        [swapped[:last], swapped[last:] + met[half_rows : half_rows + own], met[:half_rows]], axis=0
    ).astype(half)
    for part in range(out_ref.shape[0]):
        out_ref[part] = joined


def join(met, swapped, own):
    parts = met.shape[0]
    rows, columns = swapped.shape
    return pl.pallas_call(
        functools.partial(join_kernel, own),
        out_shape=jax.ShapeDtypeStruct((parts, rows + HD // 2, columns), half),
        compiler_params=pltpu.CompilerParams(vmem_limit_bytes=SMALL),
    )(met, swapped)


def bring_kernel(w_query_ref, w_key_ref, w_value_ref, after_ref, out_ref, sems):
    copies = []
    for place, ref in enumerate((w_query_ref, w_key_ref, w_value_ref)):
        copies.append(pltpu.make_async_copy(ref, out_ref.at[place], sems.at[place]))
        copies[-1].start()
    for copy in copies:
        copy.wait()


def bring(w_query, w_key, w_value, after):
    width = w_query.shape[0]
    anywhere = pl.BlockSpec(memory_space=pl.ANY)
    return pl.pallas_call(
        bring_kernel,
        in_specs=[anywhere] * 4,
        out_specs=anywhere,
        out_shape=jax.ShapeDtypeStruct((3, width, width), half),
        scratch_shapes=[pltpu.SemaphoreType.DMA((3,))],
        compiler_params=pltpu.CompilerParams(vmem_limit_bytes=SMALL),
        cost_estimate=pl.CostEstimate(flops=0, bytes_accessed=12 * width * width, transcendentals=0),
    )(w_query, w_key, w_value, after)


def finish_kernel(
    norm, own, index_ref, sums_ref, weights_ref, query_ref, key_ref, value_ref, output_ref, encoder_ref
):
    parts = sums_ref.shape[0]
    edge = HD + own
    last = edge + HD // 2
    high = last + own
    index = index_ref[0]

    def unpack(part):
        piece = sums_ref[(index - part + parts) % parts].astype(full)
        met = sums_ref[part].astype(full)
        value = jnp.concatenate([piece[edge:last, :HD], piece[edge:last, HD:]], axis=0)
        output = jnp.concatenate([met[high:, :HD], met[high:, HD:]], axis=0)
        weights = (piece[:HD, :HD], piece[:HD, HD:], value, output)
        terms = (piece[HD:edge, :HD], piece[HD:edge, HD:], piece[last:high, :HD], met[last:high, HD:])
        return weights, terms

    all_terms = ([], [], [], [])
    for pair in range(parts // 2):
        first, second = unpack(2 * pair), unpack(2 * pair + 1)
        columns = slice(2 * pair * HD, (2 * pair + 2) * HD)
        for place, out in enumerate((query_ref, key_ref, value_ref, output_ref)):
            out[:, columns] = jnp.concatenate([first[0][place], second[0][place]], axis=1) * norm
            all_terms[place].extend((first[1][place], second[1][place]))
    encoder = jnp.concatenate(all_terms[3], axis=1)
    for place in range(3):
        encoder += dot_nt(weights_ref[place], jnp.concatenate(all_terms[place], axis=1).astype(half)).T
    encoder_ref[...] = encoder * norm


def finish(index, sums, weights, norm, own):
    width = weights.shape[1]
    return pl.pallas_call(
        functools.partial(finish_kernel, norm, own),
        grid_spec=pltpu.PrefetchScalarGridSpec(
            num_scalar_prefetch=1,
            grid=(1,),
            in_specs=[whole(*sums.shape), whole(*weights.shape)],
            out_specs=[whole(HD, width)] * 4 + [whole(own, width)],
        ),
        out_shape=[jax.ShapeDtypeStruct((HD, width), full)] * 4 + [jax.ShapeDtypeStruct((own, width), full)],
        compiler_params=pltpu.CompilerParams(vmem_limit_bytes=ROOM),
    )(index, sums, weights)


def exchange(array, axis):
    return lax.all_to_all(array, axis, split_axis=0, concat_axis=0, tiled=True)


def per_device(
    grid_fields,
    cotangent,
    encoder_source,
    encoder_target,
    encoder_count,
    mesh_source,
    mesh_target,
    mesh_count,
    w_encoder,
    w_query,
    w_key,
    w_value,
    w_output,
):
    model_size = lax.axis_size("mp")
    data_size = lax.axis_size("dp")
    model_index = lax.axis_index("mp")
    local_grid = grid_fields[0]
    local_cot = cotangent[0]
    points, channels = local_grid.shape
    node_rows, width = local_cot.shape
    nodes = node_rows * model_size
    own_channels = channels // model_size

    other = lax.ppermute(local_cot, "mp", [(i, i ^ 1) for i in range(model_size)])

    partials = encoder_partials(
        local_grid,
        encoder_source,
        encoder_target,
        encoder_count,
        (model_index * points).reshape(1).astype(jnp.int32),
        w_output,
        local_cot,
    )
    received = exchange(partials, "mp")
    copies, both = collect((model_index % 2).reshape(1).astype(jnp.int32), received, local_cot, other)
    encoded = exchange(copies, "mp")
    lanes = [list(range(first, model_size, 2)) for first in range(2)]
    all_cot = lax.all_gather(both, "mp", axis=0, tiled=True, axis_index_groups=lanes)

    pairs = edge_counts(mesh_source, mesh_target, mesh_count, nodes)
    place = model_index.reshape(1).astype(jnp.int32)
    left, grads = attention(
        place,
        encoded,
        w_encoder,
        w_query,
        w_key,
        w_value,
        received,
        pairs,
        data_size,
    )

    shares = exchange(grads, "dp")
    share = jnp.sum(shares.astype(full), axis=0).astype(half)
    across = [
        (data * model_size + model, data * model_size + (model + data) % model_size)
        for data in range(data_size)
        for model in range(model_size)
    ]
    swapped = lax.ppermute(share, ("dp", "mp"), across)
    met = exchange(meet(left, all_cot, data_size, own_channels), "dp")
    joined = join(met, swapped, own_channels)
    weights = bring(w_query, w_key, w_value, joined)
    sums = exchange(joined, "dp")
    norm = 1.0 / math.sqrt(data_size * nodes)
    return tuple(finish(place, sums, weights, norm, own_channels))


def solution(mesh):
    in_specs = (
        P("dp", "mp", None),
        P("dp", "mp", None),
        P(),
        P(),
        P(),
        P(),
        P(),
        P(),
        P(),
        P(),
        P(),
        P(),
        P(),
    )
    out_specs = (P("mp", None), P("mp", None), P("mp", None), P("mp", None), P("mp", None))
    return jax.shard_map(
        per_device, mesh=mesh, in_specs=in_specs, out_specs=out_specs, check_vma=False
    )
```

```python
import functools
import math

import jax
import jax.numpy as jnp
from jax import lax
from jax.experimental import pallas as pl
from jax.experimental.pallas import tpu as pltpu
from jax.sharding import PartitionSpec as P

BLOCK = 128
HD = 64
LOW = 256
FIRST_SLOTS = 1024
EDGE_BLOCKS = 4
DEST_TILE = 256
ROW_CHUNK = 256
MEET_TILES = 4
WIDE = 60 * 1024 * 1024
SMALL = 12 * 1024 * 1024
ROOM = 24 * 1024 * 1024
half = jnp.bfloat16
full = jnp.float32


def dot_nn(left, right):
    return lax.dot_general(left, right, (((1,), (0,)), ((), ())), preferred_element_type=full)


def dot_nt(left, right):
    return lax.dot_general(left, right, (((1,), (1,)), ((), ())), preferred_element_type=full)


def whole(*shape):
    return pl.BlockSpec(shape, lambda *_: (0,) * len(shape))


def one_hot(rows, index):
    place = lax.broadcasted_iota(jnp.int16, (rows, index.shape[1]), 0)
    one, zero = jnp.asarray(1.0, half), jnp.asarray(0.0, half)
    return jnp.where(place == index.astype(jnp.int16), one, zero).astype(jnp.float8_e4m3fn)


def encoder_kernel(
    count_ref, base_ref, source_ref, target_ref, grid_ref, w_output_ref, cot_ref, out_ref, pairs_ref, w_s, sem
):
    blocks = source_ref.shape[0]
    points = grid_ref.shape[0]
    highs = points // LOW
    base = base_ref[0]
    fetch = pltpu.make_async_copy(w_output_ref, w_s, sem)
    fetch.start()

    def pair_counts(block, first):
        source = source_ref[block : block + 1, pl.ds(first, FIRST_SLOTS)] - base
        target = target_ref[block : block + 1, pl.ds(first, FIRST_SLOTS)]
        slot = first + lax.broadcasted_iota(jnp.int32, (1, FIRST_SLOTS), 1)
        used = (slot < count_ref[block]) & (source >= 0) & (source < points)
        column = jnp.where(used, lax.shift_right_logical(source, 8) * BLOCK + target, -1)
        return dot_nt(one_hot(highs * BLOCK, column), one_hot(LOW, source & (LOW - 1)))

    for block in range(blocks):
        pairs_ref[block] = pair_counts(block, 0)
    for block in range(blocks):

        def more(step, carry, block=block):
            pairs_ref[block] += pair_counts(block, pl.multiple_of(step * FIRST_SLOTS, FIRST_SLOTS))
            return carry

        lax.fori_loop(1, (count_ref[block] + FIRST_SLOTS - 1) // FIRST_SLOTS, more, 0)
    for block in range(blocks):
        counts = pairs_ref[block].astype(half)
        sums = dot_nn(counts[:BLOCK], grid_ref[:LOW])
        for high in range(1, highs):
            sums += dot_nn(
                counts[high * BLOCK : (high + 1) * BLOCK], grid_ref[high * LOW : (high + 1) * LOW]
            )
        out_ref[block, :BLOCK, :] = sums.astype(half)
    fetch.wait()
    mixed = dot_nt(w_s[...], cot_ref[...]).astype(half)
    heads = mixed.shape[0] // blocks
    for block in range(blocks):
        out_ref[block, BLOCK:, :] = mixed[block * heads : (block + 1) * heads]


def encoder_partials(local_grid, source, target, count, base, w_output, local_cot):
    blocks, slots = source.shape
    points, channels = local_grid.shape
    node_rows, width = local_cot.shape
    head_rows = width // blocks
    return pl.pallas_call(
        encoder_kernel,
        grid_spec=pltpu.PrefetchScalarGridSpec(
            num_scalar_prefetch=2,
            grid=(1,),
            in_specs=[
                whole(blocks, slots),
                whole(blocks, slots),
                whole(points, channels),
                pl.BlockSpec(memory_space=pl.ANY),
                whole(node_rows, width),
            ],
            out_specs=whole(blocks, BLOCK + head_rows, channels),
            scratch_shapes=[
                pltpu.VMEM((blocks, points // LOW * BLOCK, LOW), full),
                pltpu.VMEM((width, width), half),
                pltpu.SemaphoreType.DMA,
            ],
        ),
        out_shape=jax.ShapeDtypeStruct((blocks, BLOCK + head_rows, channels), half),
        compiler_params=pltpu.CompilerParams(vmem_limit_bytes=WIDE),
        cost_estimate=pl.CostEstimate(
            flops=2 * blocks * slots * points * BLOCK, bytes_accessed=2 * points * channels, transcendentals=0
        ),
    )(count, base, source, target, local_grid, w_output, local_cot)


def collect_kernel(odd_ref, received_ref, own_ref, other_ref, copies_ref, both_ref):
    parts, rows, _ = copies_ref.shape
    total = received_ref[0, :rows, :].astype(full)
    for part in range(1, parts):
        total += received_ref[part, :rows, :].astype(full)
    total = total.astype(half)
    for part in range(parts):
        copies_ref[part] = total
    own, other = own_ref[...], other_ref[...]
    odd = odd_ref[0] == 1

    @pl.when(odd)
    def _():
        both_ref[:rows, :] = other
        both_ref[rows:, :] = own

    @pl.when(jnp.logical_not(odd))
    def _():
        both_ref[:rows, :] = own
        both_ref[rows:, :] = other


def collect(odd, received, own, other):
    parts, _, channels = received.shape
    rows, width = own.shape
    return pl.pallas_call(
        collect_kernel,
        grid_spec=pltpu.PrefetchScalarGridSpec(
            num_scalar_prefetch=1,
            grid=(1,),
            in_specs=[whole(*received.shape), whole(rows, width), whole(rows, width)],
            out_specs=[whole(parts, rows, channels), whole(2 * rows, width)],
        ),
        out_shape=[
            jax.ShapeDtypeStruct((parts, rows, channels), half),
            jax.ShapeDtypeStruct((2 * rows, width), half),
        ],
        compiler_params=pltpu.CompilerParams(vmem_limit_bytes=SMALL),
    )(odd, received, own, other)


def edges_kernel(count_ref, source_ref, target_ref, out_ref):
    slots = source_ref.shape[1]
    nodes, columns_here = out_ref.shape
    blocks = columns_here // BLOCK
    highs = nodes // LOW
    first_block = pl.program_id(0) * blocks
    slot = lax.broadcasted_iota(jnp.int32, (1, slots), 1)
    rows = lax.broadcasted_iota(jnp.int32, (LOW, BLOCK), 0)
    columns = lax.broadcasted_iota(jnp.int32, (LOW, BLOCK), 1)
    for block in range(blocks):
        source = source_ref[pl.ds(first_block + block, 1), :]
        target = target_ref[pl.ds(first_block + block, 1), :]
        used = slot < count_ref[first_block + block]
        column = jnp.where(used, lax.shift_right_logical(source, 8) * BLOCK + target, -1)
        counts = dot_nt(one_hot(LOW, source & (LOW - 1)), one_hot(highs * BLOCK, column))
        for high in range(highs):
            own = jnp.where(high * LOW + rows == (first_block + block) * BLOCK + columns, 1.0, 0.0)
            out_ref[high * LOW : (high + 1) * LOW, block * BLOCK : (block + 1) * BLOCK] = (
                counts[:, high * BLOCK : (high + 1) * BLOCK] + own
            ).astype(half)


def edge_counts(source, target, count, nodes):
    blocks, slots = source.shape
    some = EDGE_BLOCKS
    return pl.pallas_call(
        edges_kernel,
        grid_spec=pltpu.PrefetchScalarGridSpec(
            num_scalar_prefetch=1,
            grid=(blocks // some,),
            in_specs=[
                whole(blocks, slots),
                whole(blocks, slots),
            ],
            out_specs=pl.BlockSpec((nodes, some * BLOCK), lambda b, *_: (0, b)),
        ),
        out_shape=jax.ShapeDtypeStruct((nodes, nodes), half),
        compiler_params=pltpu.CompilerParams(vmem_limit_bytes=WIDE),
        cost_estimate=pl.CostEstimate(
            flops=2 * nodes * blocks * slots * BLOCK * 2, bytes_accessed=2 * nodes * nodes, transcendentals=0
        ),
    )(count, source, target)


def attention_kernel(
    index_ref,
    encoded_ref,
    w_encoder_ref,
    w_query_ref,
    w_key_ref,
    w_value_ref,
    received_ref,
    pairs_ref,
    left_ref,
    grads_ref,
    hidden_s,
    query_s,
    key_value_s,
    queryt_s,
    keyt_s,
    valuet_s,
    gradt_s,
    expo_s,
    dattn_s,
    grad_qt_s,
    grad_kv_s,
):
    step = pl.program_id(0)
    blocks, block_rows, channels = encoded_ref.shape
    nodes = blocks * block_rows
    width = w_encoder_ref.shape[1]
    factor = 1.0 / math.sqrt(HD)

    @pl.when(step == 0)
    def _():
        encoded = encoded_ref[...].reshape(nodes, channels)
        odd = index_ref[0] % 2 == 1
        w_head = jnp.concatenate(
            [jnp.where(odd, ref[:, HD:], ref[:, :HD]) for ref in (w_query_ref, w_key_ref, w_value_ref)], axis=1
        )
        for index in range(nodes // ROW_CHUNK):
            rows = slice(index * ROW_CHUNK, (index + 1) * ROW_CHUNK)
            hidden = dot_nn(encoded[rows], w_encoder_ref[...]).astype(half)
            hidden_s[rows, :] = hidden
            mixed = dot_nn(hidden, w_head)
            query_s[rows, :] = mixed[:, :HD].astype(half)
            key_value_s[rows, :] = mixed[:, HD:].astype(half)
            flipped = mixed.T
            queryt_s[:, rows] = (flipped[:HD, :] * factor).astype(half)
            keyt_s[:, rows] = (flipped[HD : 2 * HD, :] * factor).astype(half)
            valuet_s[:, rows] = flipped[2 * HD :, :].astype(half)
        for block in range(blocks):
            gradt_s[:, block * block_rows : (block + 1) * block_rows] = received_ref[block]
        grad_kv_s[...] = jnp.zeros_like(grad_kv_s)

    dest = pl.ds(pl.multiple_of(step * DEST_TILE, DEST_TILE), DEST_TILE)
    queryt, gradt = queryt_s[:, dest], gradt_s[:, dest]
    query, grad = query_s[dest, :], gradt.astype(full).T.astype(half)
    none = jnp.zeros((DEST_TILE, HD), half)
    sides = jnp.concatenate([jnp.concatenate([query, none], axis=1), jnp.concatenate([none, grad], axis=1)], axis=0)
    empty = jnp.zeros((HD, DEST_TILE), half)
    wide = jnp.concatenate([jnp.concatenate([queryt, empty], axis=1), jnp.concatenate([empty, gradt], axis=1)], axis=0)
    total = jnp.zeros((8, DEST_TILE), full)
    weighted = jnp.zeros((8, DEST_TILE), full)
    for index in range(nodes // ROW_CHUNK):
        rows = slice(index * ROW_CHUNK, (index + 1) * ROW_CHUNK)
        both = dot_nn(key_value_s[rows, :], wide)
        score = both[:, :DEST_TILE]
        times = pairs_ref[rows, :].astype(full)
        expo = jnp.where(times > 0.0, jnp.exp(score), 0.0) * times
        dattn = both[:, DEST_TILE:]
        expo_s[rows, :] = expo
        dattn_s[rows, :] = dattn
        total += jnp.sum(expo.reshape(-1, 8, DEST_TILE), axis=0)
        weighted += jnp.sum((expo * dattn).reshape(-1, 8, DEST_TILE), axis=0)
    inverse = 1.0 / jnp.sum(total, axis=0, keepdims=True)
    mean_grad = jnp.sum(weighted, axis=0, keepdims=True) * inverse
    attended = jnp.zeros((HD, DEST_TILE), full)
    grad_qt = jnp.zeros((HD, DEST_TILE), full)
    for index in range(nodes // ROW_CHUNK):
        rows = slice(index * ROW_CHUNK, (index + 1) * ROW_CHUNK)
        attn = expo_s[rows, :] * inverse
        attn_round = attn.astype(half)
        dscore = (attn * (dattn_s[rows, :] - mean_grad)).astype(half)
        attended += dot_nn(valuet_s[:, rows], attn_round)
        grad_qt += dot_nn(keyt_s[:, rows], dscore)
        grad_kv_s[rows, :] += dot_nn(jnp.concatenate([dscore, attn_round], axis=1), sides)
    own = channels // grads_ref.shape[0]
    spare = left_ref.shape[0] - HD
    channel = lax.broadcasted_iota(jnp.int32, (spare, channels), 1)
    row = lax.broadcasted_iota(jnp.int32, (spare, channels), 0)
    pick = (channel == index_ref[0] * own + row) & (row < own)
    pair = DEST_TILE // block_rows
    here = encoded_ref[pl.ds(step * pair, pair)].reshape(DEST_TILE, channels)
    picked = dot_nt(jnp.where(pick, 1.0, 0.0).astype(half), here)
    left_ref[...] = jnp.concatenate([attended, picked], axis=0).astype(half)
    grad_qt_s[:, dest] = grad_qt.astype(half)

    @pl.when(step == pl.num_programs(0) - 1)
    def _():
        grad_kvt = grad_kv_s[...].T
        gradst = jnp.concatenate(
            [grad_qt_s[...], (grad_kvt[:HD] * factor).astype(half), grad_kvt[HD:].astype(half)], axis=0
        )
        parts = grads_ref.shape[0]
        weights = dot_nn(gradst, hidden_s[...]).T
        terms = dot_nn(gradst, encoded_ref[...].reshape(nodes, channels)).T
        piece = width // parts
        for part in range(parts):
            weight = weights[part * piece : (part + 1) * piece, :]
            term = terms[part * own : (part + 1) * own, :]
            grads_ref[(part - index_ref[0] + parts) % parts] = jnp.concatenate(
                [
                    weight[:, : 2 * HD],
                    term[:, : 2 * HD],
                    jnp.concatenate([weight[: piece // 2, 2 * HD :], weight[piece // 2 :, 2 * HD :]], axis=1),
                    jnp.concatenate([term[:, 2 * HD :], jnp.zeros((own, HD), full)], axis=1),
                ],
                axis=0,
            ).astype(half)


def attention(index, encoded, w_encoder, w_query, w_key, w_value, received, pairs, parts):
    blocks, block_rows, channels = encoded.shape
    nodes = blocks * block_rows
    width = w_encoder.shape[1]
    own = channels // parts
    left_rows = HD + 2 * own
    rows = HD + own + HD // 2 + own
    return pl.pallas_call(
        attention_kernel,
        grid_spec=pltpu.PrefetchScalarGridSpec(
            num_scalar_prefetch=1,
            grid=(nodes // DEST_TILE,),
            in_specs=[
                whole(blocks, block_rows, channels),
                whole(channels, width),
                pl.BlockSpec((width, 2 * HD), lambda j, m: (0, m[0] // 2)),
                pl.BlockSpec((width, 2 * HD), lambda j, m: (0, m[0] // 2)),
                pl.BlockSpec((width, 2 * HD), lambda j, m: (0, m[0] // 2)),
                pl.BlockSpec((blocks, HD, block_rows), lambda j, *_: (0, block_rows // HD, 0)),
                pl.BlockSpec((nodes, DEST_TILE), lambda j, *_: (0, j)),
            ],
            out_specs=[
                pl.BlockSpec((left_rows, DEST_TILE), lambda j, *_: (0, j)),
                whole(parts, rows, 2 * HD),
            ],
            scratch_shapes=[
                pltpu.VMEM((nodes, width), half),
                pltpu.VMEM((nodes, HD), half),
                pltpu.VMEM((nodes, 2 * HD), half),
                pltpu.VMEM((HD, nodes), half),
                pltpu.VMEM((HD, nodes), half),
                pltpu.VMEM((HD, nodes), half),
                pltpu.VMEM((HD, nodes), half),
                pltpu.VMEM((nodes, DEST_TILE), full),
                pltpu.VMEM((nodes, DEST_TILE), full),
                pltpu.VMEM((HD, nodes), half),
                pltpu.VMEM((nodes, 2 * HD), full),
            ],
        ),
        out_shape=[
            jax.ShapeDtypeStruct((left_rows, nodes), half),
            jax.ShapeDtypeStruct((parts, rows, 2 * HD), half),
        ],
        compiler_params=pltpu.CompilerParams(vmem_limit_bytes=WIDE),
        cost_estimate=pl.CostEstimate(
            flops=12 * nodes * nodes * HD, bytes_accessed=2 * nodes * nodes, transcendentals=nodes * nodes
        ),
    )(index, encoded, w_encoder, w_query, w_key, w_value, received, pairs)


def meet_kernel(own, left_ref, cot_ref, out_ref, cot_s, sems):
    nodes, width = cot_ref.shape
    some = nodes // MEET_TILES
    copies = []
    for tile in range(MEET_TILES):
        rows = pl.ds(tile * some, some)
        copies.append(pltpu.make_async_copy(cot_ref.at[rows, :], cot_s.at[rows, :], sems.at[tile]))
        copies[-1].start()
    met = jnp.zeros((left_ref.shape[0], width), full)
    for tile in range(MEET_TILES):
        copies[tile].wait()
        rows = slice(tile * some, (tile + 1) * some)
        met += dot_nn(left_ref[:, rows], cot_s[rows, :])
    parts, rows, columns = out_ref.shape
    piece = width // parts
    spare = rows - HD // 2 - own
    for part in range(parts):
        mine = met[:, part * piece : (part + 1) * piece]
        out_ref[part] = jnp.concatenate(
            [
                jnp.concatenate([mine[: HD // 2], mine[HD // 2 : HD]], axis=1),
                jnp.concatenate([jnp.zeros((own, piece), full), mine[HD : HD + own]], axis=1),
                jnp.zeros((spare, columns), full),
            ],
            axis=0,
        ).astype(half)


def meet(left, all_cot, parts, own):
    rows, nodes = left.shape
    width = all_cot.shape[1]
    out_rows = HD // 2 + 2 * own
    return pl.pallas_call(
        functools.partial(meet_kernel, own),
        grid=(1,),
        in_specs=[whole(rows, nodes), pl.BlockSpec(memory_space=pl.ANY)],
        out_specs=whole(parts, out_rows, 2 * HD),
        out_shape=jax.ShapeDtypeStruct((parts, out_rows, 2 * HD), half),
        scratch_shapes=[pltpu.VMEM((nodes, width), half), pltpu.SemaphoreType.DMA((MEET_TILES,))],
        compiler_params=pltpu.CompilerParams(vmem_limit_bytes=WIDE),
        cost_estimate=pl.CostEstimate(
            flops=2 * rows * nodes * width, bytes_accessed=2 * nodes * width, transcendentals=0
        ),
    )(left, all_cot)


def add_parts(ref):
    total = ref[0].astype(full)
    for part in range(1, ref.shape[0]):
        total += ref[part].astype(full)
    return total


def join_kernel(own, met_ref, swapped_ref, out_ref):
    met = add_parts(met_ref)
    swapped = swapped_ref[...].astype(full)
    half_rows = HD // 2
    last = swapped.shape[0] - own
    joined = jnp.concatenate(
        [swapped[:last], swapped[last:] + met[half_rows : half_rows + own], met[:half_rows]], axis=0
    ).astype(half)
    for part in range(out_ref.shape[0]):
        out_ref[part] = joined


def join(met, swapped, own):
    parts = met.shape[0]
    rows, columns = swapped.shape
    return pl.pallas_call(
        functools.partial(join_kernel, own),
        out_shape=jax.ShapeDtypeStruct((parts, rows + HD // 2, columns), half),
        compiler_params=pltpu.CompilerParams(vmem_limit_bytes=SMALL),
    )(met, swapped)


def bring_kernel(w_query_ref, w_key_ref, w_value_ref, after_ref, out_ref, sems):
    copies = []
    for place, ref in enumerate((w_query_ref, w_key_ref, w_value_ref)):
        copies.append(pltpu.make_async_copy(ref, out_ref.at[place], sems.at[place]))
        copies[-1].start()
    for copy in copies:
        copy.wait()


def bring(w_query, w_key, w_value, after):
    width = w_query.shape[0]
    anywhere = pl.BlockSpec(memory_space=pl.ANY)
    return pl.pallas_call(
        bring_kernel,
        in_specs=[anywhere] * 4,
        out_specs=anywhere,
        out_shape=jax.ShapeDtypeStruct((3, width, width), half),
        scratch_shapes=[pltpu.SemaphoreType.DMA((3,))],
        compiler_params=pltpu.CompilerParams(vmem_limit_bytes=SMALL),
        cost_estimate=pl.CostEstimate(flops=0, bytes_accessed=12 * width * width, transcendentals=0),
    )(w_query, w_key, w_value, after)


def finish_kernel(
    norm, own, index_ref, sums_ref, weights_ref, query_ref, key_ref, value_ref, output_ref, encoder_ref
):
    parts = sums_ref.shape[0]
    edge = HD + own
    last = edge + HD // 2
    high = last + own
    index = index_ref[0]

    def unpack(part):
        piece = sums_ref[(index - part + parts) % parts].astype(full)
        met = sums_ref[part].astype(full)
        value = jnp.concatenate([piece[edge:last, :HD], piece[edge:last, HD:]], axis=0)
        output = jnp.concatenate([met[high:, :HD], met[high:, HD:]], axis=0)
        weights = (piece[:HD, :HD], piece[:HD, HD:], value, output)
        terms = (piece[HD:edge, :HD], piece[HD:edge, HD:], piece[last:high, :HD], met[last:high, HD:])
        return weights, terms

    all_terms = ([], [], [], [])
    for pair in range(parts // 2):
        first, second = unpack(2 * pair), unpack(2 * pair + 1)
        columns = slice(2 * pair * HD, (2 * pair + 2) * HD)
        for place, out in enumerate((query_ref, key_ref, value_ref, output_ref)):
            out[:, columns] = jnp.concatenate([first[0][place], second[0][place]], axis=1) * norm
            all_terms[place].extend((first[1][place], second[1][place]))
    encoder = jnp.concatenate(all_terms[3], axis=1)
    for place in range(3):
        encoder += dot_nt(weights_ref[place], jnp.concatenate(all_terms[place], axis=1).astype(half)).T
    encoder_ref[...] = encoder * norm


def finish(index, sums, weights, norm, own):
    width = weights.shape[1]
    return pl.pallas_call(
        functools.partial(finish_kernel, norm, own),
        grid_spec=pltpu.PrefetchScalarGridSpec(
            num_scalar_prefetch=1,
            grid=(1,),
            in_specs=[whole(*sums.shape), whole(*weights.shape)],
            out_specs=[whole(HD, width)] * 4 + [whole(own, width)],
        ),
        out_shape=[jax.ShapeDtypeStruct((HD, width), full)] * 4 + [jax.ShapeDtypeStruct((own, width), full)],
        compiler_params=pltpu.CompilerParams(vmem_limit_bytes=ROOM),
    )(index, sums, weights)


def exchange(array, axis):
    return lax.all_to_all(array, axis, split_axis=0, concat_axis=0, tiled=True)


def per_device(
    grid_fields,
    cotangent,
    encoder_source,
    encoder_target,
    encoder_count,
    mesh_source,
    mesh_target,
    mesh_count,
    w_encoder,
    w_query,
    w_key,
    w_value,
    w_output,
):
    model_size = lax.axis_size("mp")
    data_size = lax.axis_size("dp")
    model_index = lax.axis_index("mp")
    local_grid = grid_fields[0]
    local_cot = cotangent[0]
    points, channels = local_grid.shape
    node_rows, width = local_cot.shape
    nodes = node_rows * model_size
    own_channels = channels // model_size

    other = lax.ppermute(local_cot, "mp", [(i, i ^ 1) for i in range(model_size)])

    partials = encoder_partials(
        local_grid,
        encoder_source,
        encoder_target,
        encoder_count,
        (model_index * points).reshape(1).astype(jnp.int32),
        w_output,
        local_cot,
    )
    received = exchange(partials, "mp")
    copies, both = collect((model_index % 2).reshape(1).astype(jnp.int32), received, local_cot, other)
    encoded = exchange(copies, "mp")
    lanes = [list(range(first, model_size, 2)) for first in range(2)]
    all_cot = lax.all_gather(both, "mp", axis=0, tiled=True, axis_index_groups=lanes)

    pairs = edge_counts(mesh_source, mesh_target, mesh_count, nodes)
    place = model_index.reshape(1).astype(jnp.int32)
    left, grads = attention(
        place,
        encoded,
        w_encoder,
        w_query,
        w_key,
        w_value,
        received,
        pairs,
        data_size,
    )

    shares = exchange(grads, "dp")
    share = jnp.sum(shares.astype(full), axis=0).astype(half)
    across = [
        (data * model_size + model, data * model_size + (model + data) % model_size)
        for data in range(data_size)
        for model in range(model_size)
    ]
    swapped = lax.ppermute(share, ("dp", "mp"), across)
    met = exchange(meet(left, all_cot, data_size, own_channels), "dp")
    joined = join(met, swapped, own_channels)
    weights = bring(w_query, w_key, w_value, joined)
    sums = exchange(joined, "dp")
    norm = 1.0 / math.sqrt(data_size * nodes)
    return tuple(finish(place, sums, weights, norm, own_channels))


def solution(mesh):
    in_specs = (
        P("dp", "mp", None),
        P("dp", "mp", None),
        P(),
        P(),
        P(),
        P(),
        P(),
        P(),
        P(),
        P(),
        P(),
        P(),
        P(),
    )
    out_specs = (P("mp", None), P("mp", None), P("mp", None), P("mp", None), P("mp", None))
    return jax.shard_map(
        per_device, mesh=mesh, in_specs=in_specs, out_specs=out_specs, check_vma=False
    )
```

```python
import functools
import math

import jax
import jax.numpy as jnp
from jax import lax
from jax.experimental import pallas as pl
from jax.experimental.pallas import tpu as pltpu
from jax.sharding import PartitionSpec as P

BLOCK = 128
HD = 64
LOW = 256
FIRST_SLOTS = 1024
EDGE_BLOCKS = 4
DEST_TILE = 256
ROW_CHUNK = 256
MEET_TILES = 4
WIDE = 60 * 1024 * 1024
SMALL = 12 * 1024 * 1024
half = jnp.bfloat16
full = jnp.float32


def dot_nn(left, right):
    return lax.dot_general(left, right, (((1,), (0,)), ((), ())), preferred_element_type=full)


def dot_nt(left, right):
    return lax.dot_general(left, right, (((1,), (1,)), ((), ())), preferred_element_type=full)


def whole(*shape):
    return pl.BlockSpec(shape, lambda *_: (0,) * len(shape))


def one_hot(rows, index):
    place = lax.broadcasted_iota(jnp.int16, (rows, index.shape[1]), 0)
    one, zero = jnp.asarray(1.0, half), jnp.asarray(0.0, half)
    return jnp.where(place == index.astype(jnp.int16), one, zero).astype(jnp.float8_e4m3fn)


def encoder_kernel(
    count_ref, base_ref, source_ref, target_ref, grid_ref, w_output_ref, cot_ref, out_ref, pairs_ref, w_s, sem
):
    blocks = source_ref.shape[0]
    points = grid_ref.shape[0]
    highs = points // LOW
    base = base_ref[0]
    fetch = pltpu.make_async_copy(w_output_ref, w_s, sem)
    fetch.start()

    def pair_counts(block, first):
        source = source_ref[block : block + 1, pl.ds(first, FIRST_SLOTS)] - base
        target = target_ref[block : block + 1, pl.ds(first, FIRST_SLOTS)]
        slot = first + lax.broadcasted_iota(jnp.int32, (1, FIRST_SLOTS), 1)
        used = (slot < count_ref[block]) & (source >= 0) & (source < points)
        column = jnp.where(used, lax.shift_right_logical(source, 8) * BLOCK + target, -1)
        return dot_nt(one_hot(highs * BLOCK, column), one_hot(LOW, source & (LOW - 1)))

    for block in range(blocks):
        pairs_ref[block] = pair_counts(block, 0)
    for block in range(blocks):

        def more(step, carry, block=block):
            pairs_ref[block] += pair_counts(block, pl.multiple_of(step * FIRST_SLOTS, FIRST_SLOTS))
            return carry

        lax.fori_loop(1, (count_ref[block] + FIRST_SLOTS - 1) // FIRST_SLOTS, more, 0)
    for block in range(blocks):
        counts = pairs_ref[block].astype(half)
        sums = dot_nn(counts[:BLOCK], grid_ref[:LOW])
        for high in range(1, highs):
            sums += dot_nn(
                counts[high * BLOCK : (high + 1) * BLOCK], grid_ref[high * LOW : (high + 1) * LOW]
            )
        out_ref[block, :BLOCK, :] = sums.astype(half)
    fetch.wait()
    mixed = dot_nt(w_s[...], cot_ref[...]).astype(half)
    heads = mixed.shape[0] // blocks
    for block in range(blocks):
        out_ref[block, BLOCK:, :] = mixed[block * heads : (block + 1) * heads]


def encoder_partials(local_grid, source, target, count, base, w_output, local_cot):
    blocks, slots = source.shape
    points, channels = local_grid.shape
    node_rows, width = local_cot.shape
    head_rows = width // blocks
    return pl.pallas_call(
        encoder_kernel,
        grid_spec=pltpu.PrefetchScalarGridSpec(
            num_scalar_prefetch=2,
            grid=(1,),
            in_specs=[
                whole(blocks, slots),
                whole(blocks, slots),
                whole(points, channels),
                pl.BlockSpec(memory_space=pl.ANY),
                whole(node_rows, width),
            ],
            out_specs=whole(blocks, BLOCK + head_rows, channels),
            scratch_shapes=[
                pltpu.VMEM((blocks, points // LOW * BLOCK, LOW), full),
                pltpu.VMEM((width, width), half),
                pltpu.SemaphoreType.DMA,
            ],
        ),
        out_shape=jax.ShapeDtypeStruct((blocks, BLOCK + head_rows, channels), half),
        compiler_params=pltpu.CompilerParams(vmem_limit_bytes=WIDE),
        cost_estimate=pl.CostEstimate(
            flops=2 * blocks * slots * points * BLOCK, bytes_accessed=2 * points * channels, transcendentals=0
        ),
    )(count, base, source, target, local_grid, w_output, local_cot)


def collect_kernel(odd_ref, received_ref, own_ref, other_ref, copies_ref, both_ref):
    parts, rows, _ = copies_ref.shape
    total = received_ref[0, :rows, :].astype(full)
    for part in range(1, parts):
        total += received_ref[part, :rows, :].astype(full)
    total = total.astype(half)
    for part in range(parts):
        copies_ref[part] = total
    own, other = own_ref[...], other_ref[...]
    odd = odd_ref[0] == 1

    @pl.when(odd)
    def _():
        both_ref[:rows, :] = other
        both_ref[rows:, :] = own

    @pl.when(jnp.logical_not(odd))
    def _():
        both_ref[:rows, :] = own
        both_ref[rows:, :] = other


def collect(odd, received, own, other):
    parts, _, channels = received.shape
    rows, width = own.shape
    return pl.pallas_call(
        collect_kernel,
        grid_spec=pltpu.PrefetchScalarGridSpec(
            num_scalar_prefetch=1,
            grid=(1,),
            in_specs=[whole(*received.shape), whole(rows, width), whole(rows, width)],
            out_specs=[whole(parts, rows, channels), whole(2 * rows, width)],
        ),
        out_shape=[
            jax.ShapeDtypeStruct((parts, rows, channels), half),
            jax.ShapeDtypeStruct((2 * rows, width), half),
        ],
        compiler_params=pltpu.CompilerParams(vmem_limit_bytes=SMALL),
    )(odd, received, own, other)


def split(value):
    high = value.astype(half)
    return high, (value - high.astype(full)).astype(half)


def edges_kernel(
    count_ref,
    index_ref,
    source_ref,
    target_ref,
    w_encoder_ref,
    w_query_ref,
    w_key_ref,
    w_value_ref,
    out_ref,
    folded_ref,
):
    @pl.when(pl.program_id(0) == 0)
    def _():
        odd = index_ref[0] % 2 == 1
        w_head = jnp.concatenate(
            [jnp.where(odd, ref[:, HD:], ref[:, :HD]) for ref in (w_query_ref, w_key_ref, w_value_ref)], axis=1
        )
        folded_ref[...] = jnp.concatenate(split(dot_nn(w_encoder_ref[...], w_head)), axis=0)

    slots = source_ref.shape[1]
    nodes, columns_here = out_ref.shape
    blocks = columns_here // BLOCK
    highs = nodes // LOW
    first_block = pl.program_id(0) * blocks
    slot = lax.broadcasted_iota(jnp.int32, (1, slots), 1)
    rows = lax.broadcasted_iota(jnp.int32, (LOW, BLOCK), 0)
    columns = lax.broadcasted_iota(jnp.int32, (LOW, BLOCK), 1)
    for block in range(blocks):
        source = source_ref[pl.ds(first_block + block, 1), :]
        target = target_ref[pl.ds(first_block + block, 1), :]
        used = slot < count_ref[first_block + block]
        column = jnp.where(used, lax.shift_right_logical(source, 8) * BLOCK + target, -1)
        counts = dot_nt(one_hot(LOW, source & (LOW - 1)), one_hot(highs * BLOCK, column))
        for high in range(highs):
            own = jnp.where(high * LOW + rows == (first_block + block) * BLOCK + columns, 1.0, 0.0)
            out_ref[high * LOW : (high + 1) * LOW, block * BLOCK : (block + 1) * BLOCK] = (
                counts[:, high * BLOCK : (high + 1) * BLOCK] + own
            ).astype(half)


def edge_counts(source, target, count, index, w_encoder, w_query, w_key, w_value, nodes):
    blocks, slots = source.shape
    channels, width = w_encoder.shape
    some = EDGE_BLOCKS
    head = pl.BlockSpec((width, 2 * HD), lambda b, c, m: (0, m[0] // 2))
    return pl.pallas_call(
        edges_kernel,
        grid_spec=pltpu.PrefetchScalarGridSpec(
            num_scalar_prefetch=2,
            grid=(blocks // some,),
            in_specs=[whole(blocks, slots), whole(blocks, slots), whole(channels, width), head, head, head],
            out_specs=[
                pl.BlockSpec((nodes, some * BLOCK), lambda b, *_: (0, b)),
                whole(2 * channels, 3 * HD),
            ],
        ),
        out_shape=[
            jax.ShapeDtypeStruct((nodes, nodes), half),
            jax.ShapeDtypeStruct((2 * channels, 3 * HD), half),
        ],
        compiler_params=pltpu.CompilerParams(vmem_limit_bytes=WIDE),
        cost_estimate=pl.CostEstimate(
            flops=2 * nodes * blocks * slots * BLOCK * 2, bytes_accessed=2 * nodes * nodes, transcendentals=0
        ),
    )(count, index, source, target, w_encoder, w_query, w_key, w_value)


def attention_kernel(
    index_ref,
    encoded_ref,
    w_encoder_ref,
    folded_ref,
    received_ref,
    pairs_ref,
    left_ref,
    grads_ref,
    query_s,
    key_value_s,
    queryt_s,
    keyt_s,
    valuet_s,
    gradt_s,
    expo_s,
    dattn_s,
    grad_qt_s,
    grad_kv_s,
):
    step = pl.program_id(0)
    blocks, block_rows, channels = encoded_ref.shape
    nodes = blocks * block_rows
    width = w_encoder_ref.shape[1]
    factor = 1.0 / math.sqrt(HD)

    @pl.when(step == 0)
    def _():
        encoded = encoded_ref[...].reshape(nodes, channels)
        for index in range(nodes // ROW_CHUNK):
            rows = slice(index * ROW_CHUNK, (index + 1) * ROW_CHUNK)
            mixed = dot_nn(jnp.concatenate([encoded[rows], encoded[rows]], axis=1), folded_ref[...])
            query_s[rows, :] = mixed[:, :HD].astype(half)
            key_value_s[rows, :] = mixed[:, HD:].astype(half)
            flipped = mixed.T
            queryt_s[:, rows] = (flipped[:HD, :] * factor).astype(half)
            keyt_s[:, rows] = (flipped[HD : 2 * HD, :] * factor).astype(half)
            valuet_s[:, rows] = flipped[2 * HD :, :].astype(half)
        for block in range(blocks):
            gradt_s[:, block * block_rows : (block + 1) * block_rows] = received_ref[block]
        grad_kv_s[...] = jnp.zeros_like(grad_kv_s)

    dest = pl.ds(pl.multiple_of(step * DEST_TILE, DEST_TILE), DEST_TILE)
    queryt, gradt = queryt_s[:, dest], gradt_s[:, dest]
    query, grad = query_s[dest, :], gradt.astype(full).T.astype(half)
    none = jnp.zeros((DEST_TILE, HD), half)
    sides = jnp.concatenate([jnp.concatenate([query, none], axis=1), jnp.concatenate([none, grad], axis=1)], axis=0)
    empty = jnp.zeros((HD, DEST_TILE), half)
    wide = jnp.concatenate([jnp.concatenate([queryt, empty], axis=1), jnp.concatenate([empty, gradt], axis=1)], axis=0)
    total = jnp.zeros((8, DEST_TILE), full)
    weighted = jnp.zeros((8, DEST_TILE), full)
    for index in range(nodes // ROW_CHUNK):
        rows = slice(index * ROW_CHUNK, (index + 1) * ROW_CHUNK)
        both = dot_nn(key_value_s[rows, :], wide)
        score = both[:, :DEST_TILE]
        times = pairs_ref[rows, :].astype(full)
        expo = jnp.where(times > 0.0, jnp.exp(score), 0.0) * times
        dattn = both[:, DEST_TILE:]
        expo_s[rows, :] = expo
        dattn_s[rows, :] = dattn
        total += jnp.sum(expo.reshape(-1, 8, DEST_TILE), axis=0)
        weighted += jnp.sum((expo * dattn).reshape(-1, 8, DEST_TILE), axis=0)
    inverse = 1.0 / jnp.sum(total, axis=0, keepdims=True)
    mean_grad = jnp.sum(weighted, axis=0, keepdims=True) * inverse
    attended = jnp.zeros((HD, DEST_TILE), full)
    grad_qt = jnp.zeros((HD, DEST_TILE), full)
    for index in range(nodes // ROW_CHUNK):
        rows = slice(index * ROW_CHUNK, (index + 1) * ROW_CHUNK)
        attn = expo_s[rows, :] * inverse
        attn_round = attn.astype(half)
        dscore = (attn * (dattn_s[rows, :] - mean_grad)).astype(half)
        attended += dot_nn(valuet_s[:, rows], attn_round)
        grad_qt += dot_nn(keyt_s[:, rows], dscore)
        grad_kv_s[rows, :] += dot_nn(jnp.concatenate([dscore, attn_round], axis=1), sides)
    own = channels // grads_ref.shape[0]
    spare = left_ref.shape[0] - HD
    channel = lax.broadcasted_iota(jnp.int32, (spare, channels), 1)
    row = lax.broadcasted_iota(jnp.int32, (spare, channels), 0)
    pick = (channel == index_ref[0] * own + row) & (row < own)
    pair = DEST_TILE // block_rows
    here = encoded_ref[pl.ds(step * pair, pair)].reshape(DEST_TILE, channels)
    picked = dot_nt(jnp.where(pick, 1.0, 0.0).astype(half), here)
    left_ref[...] = jnp.concatenate([attended, picked], axis=0).astype(half)
    grad_qt_s[:, dest] = grad_qt.astype(half)

    @pl.when(step == pl.num_programs(0) - 1)
    def _():
        grad_kvt = grad_kv_s[...].T
        gradst = jnp.concatenate(
            [grad_qt_s[...], (grad_kvt[:HD] * factor).astype(half), grad_kvt[HD:].astype(half)], axis=0
        )
        parts = grads_ref.shape[0]
        terms = dot_nn(gradst, encoded_ref[...].reshape(nodes, channels))
        w_encoder = w_encoder_ref[...]
        weights = dot_nn(
            jnp.concatenate(split(terms), axis=1), jnp.concatenate([w_encoder, w_encoder], axis=0)
        ).T
        terms = terms.T
        piece = width // parts
        for part in range(parts):
            weight = weights[part * piece : (part + 1) * piece, :]
            term = terms[part * own : (part + 1) * own, :]
            grads_ref[(part - index_ref[0] + parts) % parts] = jnp.concatenate(
                [
                    weight[:, : 2 * HD],
                    term[:, : 2 * HD],
                    jnp.concatenate([weight[: piece // 2, 2 * HD :], weight[piece // 2 :, 2 * HD :]], axis=1),
                    jnp.concatenate([term[:, 2 * HD :], jnp.zeros((own, HD), full)], axis=1),
                ],
                axis=0,
            ).astype(half)


def attention(index, encoded, w_encoder, folded, received, pairs, parts):
    blocks, block_rows, channels = encoded.shape
    nodes = blocks * block_rows
    width = w_encoder.shape[1]
    own = channels // parts
    left_rows = HD + 2 * own
    rows = HD + own + HD // 2 + own
    return pl.pallas_call(
        attention_kernel,
        grid_spec=pltpu.PrefetchScalarGridSpec(
            num_scalar_prefetch=1,
            grid=(nodes // DEST_TILE,),
            in_specs=[
                whole(blocks, block_rows, channels),
                whole(channels, width),
                whole(*folded.shape),
                pl.BlockSpec((blocks, HD, block_rows), lambda j, *_: (0, block_rows // HD, 0)),
                pl.BlockSpec((nodes, DEST_TILE), lambda j, *_: (0, j)),
            ],
            out_specs=[
                pl.BlockSpec((left_rows, DEST_TILE), lambda j, *_: (0, j)),
                whole(parts, rows, 2 * HD),
            ],
            scratch_shapes=[
                pltpu.VMEM((nodes, HD), half),
                pltpu.VMEM((nodes, 2 * HD), half),
                pltpu.VMEM((HD, nodes), half),
                pltpu.VMEM((HD, nodes), half),
                pltpu.VMEM((HD, nodes), half),
                pltpu.VMEM((HD, nodes), half),
                pltpu.VMEM((nodes, DEST_TILE), full),
                pltpu.VMEM((nodes, DEST_TILE), full),
                pltpu.VMEM((HD, nodes), half),
                pltpu.VMEM((nodes, 2 * HD), full),
            ],
        ),
        out_shape=[
            jax.ShapeDtypeStruct((left_rows, nodes), half),
            jax.ShapeDtypeStruct((parts, rows, 2 * HD), half),
        ],
        compiler_params=pltpu.CompilerParams(vmem_limit_bytes=WIDE),
        cost_estimate=pl.CostEstimate(
            flops=12 * nodes * nodes * HD, bytes_accessed=2 * nodes * nodes, transcendentals=nodes * nodes
        ),
    )(index, encoded, w_encoder, folded, received, pairs)


def meet_kernel(own, left_any, cot_ref, out_ref, left_ref, cot_s, sems):
    nodes, width = cot_ref.shape
    some = nodes // MEET_TILES
    first = pltpu.make_async_copy(left_any, left_ref, sems.at[MEET_TILES])
    first.start()
    copies = []
    for tile in range(MEET_TILES):
        rows = pl.ds(tile * some, some)
        copies.append(pltpu.make_async_copy(cot_ref.at[rows, :], cot_s.at[rows, :], sems.at[tile]))
        copies[-1].start()
    met = jnp.zeros((left_ref.shape[0], width), full)
    first.wait()
    for tile in range(MEET_TILES):
        copies[tile].wait()
        rows = slice(tile * some, (tile + 1) * some)
        met += dot_nn(left_ref[:, rows], cot_s[rows, :])
    parts, rows, columns = out_ref.shape
    piece = width // parts
    spare = rows - HD // 2 - own
    for part in range(parts):
        mine = met[:, part * piece : (part + 1) * piece]
        out_ref[part] = jnp.concatenate(
            [
                jnp.concatenate([mine[: HD // 2], mine[HD // 2 : HD]], axis=1),
                jnp.concatenate([jnp.zeros((own, piece), full), mine[HD : HD + own]], axis=1),
                jnp.zeros((spare, columns), full),
            ],
            axis=0,
        ).astype(half)


def meet(left, all_cot, parts, own):
    rows, nodes = left.shape
    width = all_cot.shape[1]
    out_rows = HD // 2 + 2 * own
    return pl.pallas_call(
        functools.partial(meet_kernel, own),
        grid=(1,),
        in_specs=[pl.BlockSpec(memory_space=pl.ANY)] * 2,
        out_specs=whole(parts, out_rows, 2 * HD),
        out_shape=jax.ShapeDtypeStruct((parts, out_rows, 2 * HD), half),
        scratch_shapes=[
            pltpu.VMEM((rows, nodes), half),
            pltpu.VMEM((nodes, width), half),
            pltpu.SemaphoreType.DMA((MEET_TILES + 1,)),
        ],
        compiler_params=pltpu.CompilerParams(vmem_limit_bytes=WIDE),
        cost_estimate=pl.CostEstimate(
            flops=2 * rows * nodes * width, bytes_accessed=2 * nodes * width, transcendentals=0
        ),
    )(left, all_cot)


def add_parts(ref):
    total = ref[0].astype(full)
    for part in range(1, ref.shape[0]):
        total += ref[part].astype(full)
    return total


def join_kernel(own, met_ref, swapped_ref, out_ref):
    met = add_parts(met_ref)
    swapped = swapped_ref[...].astype(full)
    half_rows = HD // 2
    last = swapped.shape[0] - own
    joined = jnp.concatenate(
        [swapped[:last], swapped[last:] + met[half_rows : half_rows + own], met[:half_rows]], axis=0
    ).astype(half)
    for part in range(out_ref.shape[0]):
        out_ref[part] = joined


def join(met, swapped, own):
    parts = met.shape[0]
    rows, columns = swapped.shape
    return pl.pallas_call(
        functools.partial(join_kernel, own),
        out_shape=jax.ShapeDtypeStruct((parts, rows + HD // 2, columns), half),
        compiler_params=pltpu.CompilerParams(vmem_limit_bytes=SMALL),
    )(met, swapped)


def finish_kernel(
    norm,
    own,
    index_ref,
    sums_ref,
    w_query_ref,
    w_key_ref,
    w_value_ref,
    query_ref,
    key_ref,
    value_ref,
    output_ref,
    encoder_ref,
    weights_ref,
    sems,
):
    copies = []
    for place, ref in enumerate((w_query_ref, w_key_ref, w_value_ref)):
        copies.append(pltpu.make_async_copy(ref, weights_ref.at[place], sems.at[place]))
        copies[-1].start()
    parts = sums_ref.shape[0]
    edge = HD + own
    last = edge + HD // 2
    high = last + own
    index = index_ref[0]

    def unpack(part):
        piece = sums_ref[(index - part + parts) % parts].astype(full)
        met = sums_ref[part].astype(full)
        value = jnp.concatenate([piece[edge:last, :HD], piece[edge:last, HD:]], axis=0)
        output = jnp.concatenate([met[high:, :HD], met[high:, HD:]], axis=0)
        weights = (piece[:HD, :HD], piece[:HD, HD:], value, output)
        terms = (piece[HD:edge, :HD], piece[HD:edge, HD:], piece[last:high, :HD], met[last:high, HD:])
        return weights, terms

    all_terms = ([], [], [], [])
    for pair in range(parts // 2):
        first, second = unpack(2 * pair), unpack(2 * pair + 1)
        columns = slice(2 * pair * HD, (2 * pair + 2) * HD)
        for place, out in enumerate((query_ref, key_ref, value_ref, output_ref)):
            out[:, columns] = jnp.concatenate([first[0][place], second[0][place]], axis=1) * norm
            all_terms[place].extend((first[1][place], second[1][place]))
    encoder = jnp.concatenate(all_terms[3], axis=1)
    for place in range(3):
        copies[place].wait()
        encoder += dot_nt(jnp.concatenate(all_terms[place], axis=1).astype(half), weights_ref[place])
    encoder_ref[...] = encoder * norm


def finish(index, sums, w_query, w_key, w_value, norm, own):
    width = w_query.shape[0]
    return pl.pallas_call(
        functools.partial(finish_kernel, norm, own),
        grid_spec=pltpu.PrefetchScalarGridSpec(
            num_scalar_prefetch=1,
            grid=(1,),
            in_specs=[whole(*sums.shape)] + [pl.BlockSpec(memory_space=pl.ANY)] * 3,
            out_specs=[whole(HD, width)] * 4 + [whole(own, width)],
            scratch_shapes=[
                pltpu.VMEM((3, width, width), half),
                pltpu.SemaphoreType.DMA((3,)),
            ],
        ),
        out_shape=[jax.ShapeDtypeStruct((HD, width), full)] * 4 + [jax.ShapeDtypeStruct((own, width), full)],
        compiler_params=pltpu.CompilerParams(vmem_limit_bytes=WIDE),
    )(index, sums, w_query, w_key, w_value)


def exchange(array, axis):
    return lax.all_to_all(array, axis, split_axis=0, concat_axis=0, tiled=True)


def per_device(
    grid_fields,
    cotangent,
    encoder_source,
    encoder_target,
    encoder_count,
    mesh_source,
    mesh_target,
    mesh_count,
    w_encoder,
    w_query,
    w_key,
    w_value,
    w_output,
):
    model_size = lax.axis_size("mp")
    data_size = lax.axis_size("dp")
    model_index = lax.axis_index("mp")
    local_grid = grid_fields[0]
    local_cot = cotangent[0]
    points, channels = local_grid.shape
    node_rows, width = local_cot.shape
    nodes = node_rows * model_size
    own_channels = channels // model_size

    other = lax.ppermute(local_cot, "mp", [(i, i ^ 1) for i in range(model_size)])

    partials = encoder_partials(
        local_grid,
        encoder_source,
        encoder_target,
        encoder_count,
        (model_index * points).reshape(1).astype(jnp.int32),
        w_output,
        local_cot,
    )
    received = exchange(partials, "mp")
    copies, both = collect((model_index % 2).reshape(1).astype(jnp.int32), received, local_cot, other)
    encoded = exchange(copies, "mp")
    lanes = [list(range(first, model_size, 2)) for first in range(2)]
    all_cot = lax.all_gather(both, "mp", axis=0, tiled=True, axis_index_groups=lanes)

    place = model_index.reshape(1).astype(jnp.int32)
    pairs, folded = edge_counts(
        mesh_source, mesh_target, mesh_count, place, w_encoder, w_query, w_key, w_value, nodes
    )
    left, grads = attention(place, encoded, w_encoder, folded, received, pairs, data_size)

    shares = exchange(grads, "dp")
    share = jnp.sum(shares.astype(full), axis=0).astype(half)
    across = [
        (data * model_size + model, data * model_size + (model + data) % model_size)
        for data in range(data_size)
        for model in range(model_size)
    ]
    swapped = lax.ppermute(share, ("dp", "mp"), across)
    met = exchange(meet(left, all_cot, data_size, own_channels), "dp")
    sums = exchange(join(met, swapped, own_channels), "dp")
    norm = 1.0 / math.sqrt(data_size * nodes)
    return tuple(finish(place, sums, w_query, w_key, w_value, norm, own_channels))


def solution(mesh):
    in_specs = (
        P("dp", "mp", None),
        P("dp", "mp", None),
        P(),
        P(),
        P(),
        P(),
        P(),
        P(),
        P(),
        P(),
        P(),
        P(),
        P(),
    )
    out_specs = (P("mp", None), P("mp", None), P("mp", None), P("mp", None), P("mp", None))
    return jax.shard_map(
        per_device, mesh=mesh, in_specs=in_specs, out_specs=out_specs, check_vma=False
    )
```

```python
import functools
import math

import jax
import jax.numpy as jnp
from jax import lax
from jax.experimental import pallas as pl
from jax.experimental.pallas import tpu as pltpu
from jax.sharding import PartitionSpec as P

BLOCK = 128
HD = 64
LOW = 256
FIRST_SLOTS = 1024
EDGE_BLOCKS = 4
DEST_TILE = 256
ROW_CHUNK = 256
MEET_TILES = 4
WIDE = 60 * 1024 * 1024
SMALL = 12 * 1024 * 1024
half = jnp.bfloat16
full = jnp.float32


def dot_nn(left, right):
    return lax.dot_general(left, right, (((1,), (0,)), ((), ())), preferred_element_type=full)


def dot_nt(left, right):
    return lax.dot_general(left, right, (((1,), (1,)), ((), ())), preferred_element_type=full)


def whole(*shape):
    return pl.BlockSpec(shape, lambda *_: (0,) * len(shape))


def one_hot(rows, index):
    place = lax.broadcasted_iota(jnp.int16, (rows, index.shape[1]), 0)
    one, zero = jnp.asarray(1.0, half), jnp.asarray(0.0, half)
    return jnp.where(place == index.astype(jnp.int16), one, zero).astype(jnp.float8_e4m3fn)


def encoder_kernel(
    count_ref, base_ref, source_ref, target_ref, grid_ref, w_output_ref, cot_ref, out_ref, pairs_ref, w_s, sem
):
    blocks = source_ref.shape[0]
    points = grid_ref.shape[0]
    highs = points // LOW
    base = base_ref[0]
    fetch = pltpu.make_async_copy(w_output_ref, w_s, sem)
    fetch.start()

    def pair_counts(block, first):
        source = source_ref[block : block + 1, pl.ds(first, FIRST_SLOTS)] - base
        target = target_ref[block : block + 1, pl.ds(first, FIRST_SLOTS)]
        slot = first + lax.broadcasted_iota(jnp.int32, (1, FIRST_SLOTS), 1)
        used = (slot < count_ref[block]) & (source >= 0) & (source < points)
        column = jnp.where(used, lax.shift_right_logical(source, 8) * BLOCK + target, -1)
        return dot_nt(one_hot(highs * BLOCK, column), one_hot(LOW, source & (LOW - 1)))

    for block in range(blocks):
        pairs_ref[block] = pair_counts(block, 0)
    for block in range(blocks):

        def more(step, carry, block=block):
            pairs_ref[block] += pair_counts(block, pl.multiple_of(step * FIRST_SLOTS, FIRST_SLOTS))
            return carry

        lax.fori_loop(1, (count_ref[block] + FIRST_SLOTS - 1) // FIRST_SLOTS, more, 0)
    for block in range(blocks):
        counts = pairs_ref[block].astype(half)
        sums = dot_nn(counts[:BLOCK], grid_ref[:LOW])
        for high in range(1, highs):
            sums += dot_nn(
                counts[high * BLOCK : (high + 1) * BLOCK], grid_ref[high * LOW : (high + 1) * LOW]
            )
        out_ref[block, :BLOCK, :] = sums.astype(half)
    fetch.wait()
    mixed = dot_nt(w_s[...], cot_ref[...]).astype(half)
    heads = mixed.shape[0] // blocks
    for block in range(blocks):
        out_ref[block, BLOCK:, :] = mixed[block * heads : (block + 1) * heads]


def encoder_partials(local_grid, source, target, count, base, w_output, local_cot):
    blocks, slots = source.shape
    points, channels = local_grid.shape
    node_rows, width = local_cot.shape
    head_rows = width // blocks
    return pl.pallas_call(
        encoder_kernel,
        grid_spec=pltpu.PrefetchScalarGridSpec(
            num_scalar_prefetch=2,
            grid=(1,),
            in_specs=[
                whole(blocks, slots),
                whole(blocks, slots),
                whole(points, channels),
                pl.BlockSpec(memory_space=pl.ANY),
                whole(node_rows, width),
            ],
            out_specs=whole(blocks, BLOCK + head_rows, channels),
            scratch_shapes=[
                pltpu.VMEM((blocks, points // LOW * BLOCK, LOW), full),
                pltpu.VMEM((width, width), half),
                pltpu.SemaphoreType.DMA,
            ],
        ),
        out_shape=jax.ShapeDtypeStruct((blocks, BLOCK + head_rows, channels), half),
        compiler_params=pltpu.CompilerParams(vmem_limit_bytes=WIDE),
        cost_estimate=pl.CostEstimate(
            flops=2 * blocks * slots * points * BLOCK, bytes_accessed=2 * points * channels, transcendentals=0
        ),
    )(count, base, source, target, local_grid, w_output, local_cot)


def collect_kernel(received_ref, copies_ref):
    parts, rows, _ = copies_ref.shape
    total = received_ref[0].astype(full)
    for part in range(1, parts):
        total += received_ref[part].astype(full)
    total = total.astype(half)
    for part in range(parts):
        copies_ref[part] = total


def collect(received, rows):
    parts, _, channels = received.shape
    return pl.pallas_call(
        collect_kernel,
        grid=(1,),
        in_specs=[whole(parts, rows, channels)],
        out_specs=whole(parts, rows, channels),
        out_shape=jax.ShapeDtypeStruct((parts, rows, channels), half),
        compiler_params=pltpu.CompilerParams(vmem_limit_bytes=SMALL),
    )(received)


def pair_kernel(odd_ref, own_ref, other_ref, both_ref):
    rows = own_ref.shape[0]
    own, other = own_ref[...], other_ref[...]
    odd = odd_ref[0] == 1

    @pl.when(odd)
    def _():
        both_ref[:rows, :] = other
        both_ref[rows:, :] = own

    @pl.when(jnp.logical_not(odd))
    def _():
        both_ref[:rows, :] = own
        both_ref[rows:, :] = other


def pair_up(odd, own, other):
    rows, width = own.shape
    return pl.pallas_call(
        pair_kernel,
        grid_spec=pltpu.PrefetchScalarGridSpec(
            num_scalar_prefetch=1,
            grid=(1,),
            in_specs=[whole(rows, width), whole(rows, width)],
            out_specs=whole(2 * rows, width),
        ),
        out_shape=jax.ShapeDtypeStruct((2 * rows, width), half),
        compiler_params=pltpu.CompilerParams(vmem_limit_bytes=SMALL),
    )(odd, own, other)


def split(value):
    high = value.astype(half)
    return high, (value - high.astype(full)).astype(half)


def edges_kernel(
    count_ref,
    index_ref,
    source_ref,
    target_ref,
    w_encoder_ref,
    w_query_ref,
    w_key_ref,
    w_value_ref,
    out_ref,
    folded_ref,
):
    @pl.when(pl.program_id(0) == 0)
    def _():
        odd = index_ref[0] % 2 == 1
        w_head = jnp.concatenate(
            [jnp.where(odd, ref[:, HD:], ref[:, :HD]) for ref in (w_query_ref, w_key_ref, w_value_ref)], axis=1
        )
        folded_ref[...] = jnp.concatenate(split(dot_nn(w_encoder_ref[...], w_head)), axis=0)

    slots = source_ref.shape[1]
    nodes, columns_here = out_ref.shape
    blocks = columns_here // BLOCK
    highs = nodes // LOW
    first_block = pl.program_id(0) * blocks
    slot = lax.broadcasted_iota(jnp.int32, (1, slots), 1)
    rows = lax.broadcasted_iota(jnp.int32, (LOW, BLOCK), 0)
    columns = lax.broadcasted_iota(jnp.int32, (LOW, BLOCK), 1)
    for block in range(blocks):
        source = source_ref[pl.ds(first_block + block, 1), :]
        target = target_ref[pl.ds(first_block + block, 1), :]
        used = slot < count_ref[first_block + block]
        column = jnp.where(used, lax.shift_right_logical(source, 8) * BLOCK + target, -1)
        counts = dot_nt(one_hot(LOW, source & (LOW - 1)), one_hot(highs * BLOCK, column))
        for high in range(highs):
            own = jnp.where(high * LOW + rows == (first_block + block) * BLOCK + columns, 1.0, 0.0)
            out_ref[high * LOW : (high + 1) * LOW, block * BLOCK : (block + 1) * BLOCK] = (
                counts[:, high * BLOCK : (high + 1) * BLOCK] + own
            ).astype(half)


def edge_counts(source, target, count, index, w_encoder, w_query, w_key, w_value, nodes):
    blocks, slots = source.shape
    channels, width = w_encoder.shape
    some = EDGE_BLOCKS
    head = pl.BlockSpec((width, 2 * HD), lambda b, c, m: (0, m[0] // 2))
    return pl.pallas_call(
        edges_kernel,
        grid_spec=pltpu.PrefetchScalarGridSpec(
            num_scalar_prefetch=2,
            grid=(blocks // some,),
            in_specs=[whole(blocks, slots), whole(blocks, slots), whole(channels, width), head, head, head],
            out_specs=[
                pl.BlockSpec((nodes, some * BLOCK), lambda b, *_: (0, b)),
                whole(2 * channels, 3 * HD),
            ],
        ),
        out_shape=[
            jax.ShapeDtypeStruct((nodes, nodes), half),
            jax.ShapeDtypeStruct((2 * channels, 3 * HD), half),
        ],
        compiler_params=pltpu.CompilerParams(vmem_limit_bytes=WIDE),
        cost_estimate=pl.CostEstimate(
            flops=2 * nodes * blocks * slots * BLOCK * 2, bytes_accessed=2 * nodes * nodes, transcendentals=0
        ),
    )(count, index, source, target, w_encoder, w_query, w_key, w_value)


def attention_kernel(
    index_ref,
    encoded_ref,
    w_encoder_ref,
    folded_ref,
    received_ref,
    pairs_ref,
    left_ref,
    grads_ref,
    query_s,
    key_value_s,
    queryt_s,
    keyt_s,
    valuet_s,
    gradt_s,
    expo_s,
    dattn_s,
    grad_qt_s,
    grad_kv_s,
):
    step = pl.program_id(0)
    blocks, block_rows, channels = encoded_ref.shape
    nodes = blocks * block_rows
    width = w_encoder_ref.shape[1]
    factor = 1.0 / math.sqrt(HD)

    @pl.when(step == 0)
    def _():
        encoded = encoded_ref[...].reshape(nodes, channels)
        for index in range(nodes // ROW_CHUNK):
            rows = slice(index * ROW_CHUNK, (index + 1) * ROW_CHUNK)
            mixed = dot_nn(jnp.concatenate([encoded[rows], encoded[rows]], axis=1), folded_ref[...])
            query_s[rows, :] = mixed[:, :HD].astype(half)
            key_value_s[rows, :] = mixed[:, HD:].astype(half)
            flipped = mixed.T
            queryt_s[:, rows] = (flipped[:HD, :] * factor).astype(half)
            keyt_s[:, rows] = (flipped[HD : 2 * HD, :] * factor).astype(half)
            valuet_s[:, rows] = flipped[2 * HD :, :].astype(half)
        for block in range(blocks):
            gradt_s[:, block * block_rows : (block + 1) * block_rows] = received_ref[block]
        grad_kv_s[...] = jnp.zeros_like(grad_kv_s)

    dest = pl.ds(pl.multiple_of(step * DEST_TILE, DEST_TILE), DEST_TILE)
    queryt, gradt = queryt_s[:, dest], gradt_s[:, dest]
    query, grad = query_s[dest, :], gradt.astype(full).T.astype(half)
    none = jnp.zeros((DEST_TILE, HD), half)
    sides = jnp.concatenate([jnp.concatenate([query, none], axis=1), jnp.concatenate([none, grad], axis=1)], axis=0)
    empty = jnp.zeros((HD, DEST_TILE), half)
    wide = jnp.concatenate([jnp.concatenate([queryt, empty], axis=1), jnp.concatenate([empty, gradt], axis=1)], axis=0)
    total = jnp.zeros((8, DEST_TILE), full)
    weighted = jnp.zeros((8, DEST_TILE), full)
    for index in range(nodes // ROW_CHUNK):
        rows = slice(index * ROW_CHUNK, (index + 1) * ROW_CHUNK)
        both = dot_nn(key_value_s[rows, :], wide)
        score = both[:, :DEST_TILE]
        times = pairs_ref[rows, :].astype(full)
        expo = jnp.where(times > 0.0, jnp.exp(score), 0.0) * times
        dattn = both[:, DEST_TILE:]
        expo_s[rows, :] = expo
        dattn_s[rows, :] = dattn
        total += jnp.sum(expo.reshape(-1, 8, DEST_TILE), axis=0)
        weighted += jnp.sum((expo * dattn).reshape(-1, 8, DEST_TILE), axis=0)
    inverse = 1.0 / jnp.sum(total, axis=0, keepdims=True)
    mean_grad = jnp.sum(weighted, axis=0, keepdims=True) * inverse
    attended = jnp.zeros((HD, DEST_TILE), full)
    grad_qt = jnp.zeros((HD, DEST_TILE), full)
    for index in range(nodes // ROW_CHUNK):
        rows = slice(index * ROW_CHUNK, (index + 1) * ROW_CHUNK)
        attn = expo_s[rows, :] * inverse
        attn_round = attn.astype(half)
        dscore = (attn * (dattn_s[rows, :] - mean_grad)).astype(half)
        attended += dot_nn(valuet_s[:, rows], attn_round)
        grad_qt += dot_nn(keyt_s[:, rows], dscore)
        grad_kv_s[rows, :] += dot_nn(jnp.concatenate([dscore, attn_round], axis=1), sides)
    own = channels // grads_ref.shape[0]
    spare = left_ref.shape[0] - HD
    channel = lax.broadcasted_iota(jnp.int32, (spare, channels), 1)
    row = lax.broadcasted_iota(jnp.int32, (spare, channels), 0)
    pick = (channel == index_ref[0] * own + row) & (row < own)
    pair = DEST_TILE // block_rows
    here = encoded_ref[pl.ds(step * pair, pair)].reshape(DEST_TILE, channels)
    picked = dot_nt(jnp.where(pick, 1.0, 0.0).astype(half), here)
    left_ref[...] = jnp.concatenate([attended, picked], axis=0).astype(half)
    grad_qt_s[:, dest] = grad_qt.astype(half)

    @pl.when(step == pl.num_programs(0) - 1)
    def _():
        grad_kvt = grad_kv_s[...].T
        gradst = jnp.concatenate(
            [grad_qt_s[...], (grad_kvt[:HD] * factor).astype(half), grad_kvt[HD:].astype(half)], axis=0
        )
        parts = grads_ref.shape[0]
        terms = dot_nn(gradst, encoded_ref[...].reshape(nodes, channels))
        w_encoder = w_encoder_ref[...]
        weights = dot_nn(
            jnp.concatenate(split(terms), axis=1), jnp.concatenate([w_encoder, w_encoder], axis=0)
        ).T
        terms = terms.T
        piece = width // parts
        for part in range(parts):
            weight = weights[part * piece : (part + 1) * piece, :]
            term = terms[part * own : (part + 1) * own, :]
            grads_ref[(part - index_ref[0] + parts) % parts] = jnp.concatenate(
                [
                    weight[:, : 2 * HD],
                    term[:, : 2 * HD],
                    jnp.concatenate([weight[: piece // 2, 2 * HD :], weight[piece // 2 :, 2 * HD :]], axis=1),
                    jnp.concatenate([term[:, 2 * HD :], jnp.zeros((own, HD), full)], axis=1),
                ],
                axis=0,
            ).astype(half)


def attention(index, encoded, w_encoder, folded, received, pairs, parts):
    blocks, block_rows, channels = encoded.shape
    nodes = blocks * block_rows
    width = w_encoder.shape[1]
    own = channels // parts
    left_rows = HD + 2 * own
    rows = HD + own + HD // 2 + own
    return pl.pallas_call(
        attention_kernel,
        grid_spec=pltpu.PrefetchScalarGridSpec(
            num_scalar_prefetch=1,
            grid=(nodes // DEST_TILE,),
            in_specs=[
                whole(blocks, block_rows, channels),
                whole(channels, width),
                whole(*folded.shape),
                pl.BlockSpec((blocks, HD, block_rows), lambda j, *_: (0, block_rows // HD, 0)),
                pl.BlockSpec((nodes, DEST_TILE), lambda j, *_: (0, j)),
            ],
            out_specs=[
                pl.BlockSpec((left_rows, DEST_TILE), lambda j, *_: (0, j)),
                whole(parts, rows, 2 * HD),
            ],
            scratch_shapes=[
                pltpu.VMEM((nodes, HD), half),
                pltpu.VMEM((nodes, 2 * HD), half),
                pltpu.VMEM((HD, nodes), half),
                pltpu.VMEM((HD, nodes), half),
                pltpu.VMEM((HD, nodes), half),
                pltpu.VMEM((HD, nodes), half),
                pltpu.VMEM((nodes, DEST_TILE), full),
                pltpu.VMEM((nodes, DEST_TILE), full),
                pltpu.VMEM((HD, nodes), half),
                pltpu.VMEM((nodes, 2 * HD), full),
            ],
        ),
        out_shape=[
            jax.ShapeDtypeStruct((left_rows, nodes), half),
            jax.ShapeDtypeStruct((parts, rows, 2 * HD), half),
        ],
        compiler_params=pltpu.CompilerParams(vmem_limit_bytes=WIDE),
        cost_estimate=pl.CostEstimate(
            flops=12 * nodes * nodes * HD, bytes_accessed=2 * nodes * nodes, transcendentals=nodes * nodes
        ),
    )(index, encoded, w_encoder, folded, received, pairs)


def meet_kernel(own, left_any, cot_ref, out_ref, left_ref, cot_s, sems):
    nodes, width = cot_ref.shape
    some = nodes // MEET_TILES
    first = pltpu.make_async_copy(left_any, left_ref, sems.at[MEET_TILES])
    first.start()
    copies = []
    for tile in range(MEET_TILES):
        rows = pl.ds(tile * some, some)
        copies.append(pltpu.make_async_copy(cot_ref.at[rows, :], cot_s.at[rows, :], sems.at[tile]))
        copies[-1].start()
    met = jnp.zeros((left_ref.shape[0], width), full)
    first.wait()
    for tile in range(MEET_TILES):
        copies[tile].wait()
        rows = slice(tile * some, (tile + 1) * some)
        met += dot_nn(left_ref[:, rows], cot_s[rows, :])
    parts, rows, columns = out_ref.shape
    piece = width // parts
    spare = rows - HD // 2 - own
    for part in range(parts):
        mine = met[:, part * piece : (part + 1) * piece]
        out_ref[part] = jnp.concatenate(
            [
                jnp.concatenate([mine[: HD // 2], mine[HD // 2 : HD]], axis=1),
                jnp.concatenate([jnp.zeros((own, piece), full), mine[HD : HD + own]], axis=1),
                jnp.zeros((spare, columns), full),
            ],
            axis=0,
        ).astype(half)


def meet(left, all_cot, parts, own):
    rows, nodes = left.shape
    width = all_cot.shape[1]
    out_rows = HD // 2 + 2 * own
    return pl.pallas_call(
        functools.partial(meet_kernel, own),
        grid=(1,),
        in_specs=[pl.BlockSpec(memory_space=pl.ANY)] * 2,
        out_specs=whole(parts, out_rows, 2 * HD),
        out_shape=jax.ShapeDtypeStruct((parts, out_rows, 2 * HD), half),
        scratch_shapes=[
            pltpu.VMEM((rows, nodes), half),
            pltpu.VMEM((nodes, width), half),
            pltpu.SemaphoreType.DMA((MEET_TILES + 1,)),
        ],
        compiler_params=pltpu.CompilerParams(vmem_limit_bytes=WIDE),
        cost_estimate=pl.CostEstimate(
            flops=2 * rows * nodes * width, bytes_accessed=2 * nodes * width, transcendentals=0
        ),
    )(left, all_cot)


def add_parts(ref):
    total = ref[0].astype(full)
    for part in range(1, ref.shape[0]):
        total += ref[part].astype(full)
    return total


def join_kernel(own, met_ref, swapped_ref, out_ref):
    met = add_parts(met_ref)
    swapped = swapped_ref[...].astype(full)
    half_rows = HD // 2
    last = swapped.shape[0] - own
    joined = jnp.concatenate(
        [swapped[:last], swapped[last:] + met[half_rows : half_rows + own], met[:half_rows]], axis=0
    ).astype(half)
    for part in range(out_ref.shape[0]):
        out_ref[part] = joined


def join(met, swapped, own, parts):
    rows, columns = swapped.shape
    return pl.pallas_call(
        functools.partial(join_kernel, own),
        out_shape=jax.ShapeDtypeStruct((parts, rows + HD // 2, columns), half),
        compiler_params=pltpu.CompilerParams(vmem_limit_bytes=SMALL),
    )(met, swapped)


def finish_kernel(
    norm,
    own,
    index_ref,
    sums_ref,
    w_query_ref,
    w_key_ref,
    w_value_ref,
    query_ref,
    key_ref,
    value_ref,
    output_ref,
    encoder_ref,
    weights_ref,
    sems,
):
    copies = []
    for place, ref in enumerate((w_query_ref, w_key_ref, w_value_ref)):
        copies.append(pltpu.make_async_copy(ref, weights_ref.at[place], sems.at[place]))
        copies[-1].start()
    parts = sums_ref.shape[0]
    edge = HD + own
    last = edge + HD // 2
    high = last + own
    index = index_ref[0]

    def unpack(part):
        piece = sums_ref[(index - part + parts) % parts].astype(full)
        met = sums_ref[part].astype(full)
        value = jnp.concatenate([piece[edge:last, :HD], piece[edge:last, HD:]], axis=0)
        output = jnp.concatenate([met[high:, :HD], met[high:, HD:]], axis=0)
        weights = (piece[:HD, :HD], piece[:HD, HD:], value, output)
        terms = (piece[HD:edge, :HD], piece[HD:edge, HD:], piece[last:high, :HD], met[last:high, HD:])
        return weights, terms

    all_terms = ([], [], [], [])
    for pair in range(parts // 2):
        first, second = unpack(2 * pair), unpack(2 * pair + 1)
        columns = slice(2 * pair * HD, (2 * pair + 2) * HD)
        for place, out in enumerate((query_ref, key_ref, value_ref, output_ref)):
            out[:, columns] = jnp.concatenate([first[0][place], second[0][place]], axis=1) * norm
            all_terms[place].extend((first[1][place], second[1][place]))
    encoder = jnp.concatenate(all_terms[3], axis=1)
    for place in range(3):
        copies[place].wait()
        encoder += dot_nt(jnp.concatenate(all_terms[place], axis=1).astype(half), weights_ref[place])
    encoder_ref[...] = encoder * norm


def finish(index, sums, w_query, w_key, w_value, norm, own):
    width = w_query.shape[0]
    return pl.pallas_call(
        functools.partial(finish_kernel, norm, own),
        grid_spec=pltpu.PrefetchScalarGridSpec(
            num_scalar_prefetch=1,
            grid=(1,),
            in_specs=[whole(*sums.shape)] + [pl.BlockSpec(memory_space=pl.ANY)] * 3,
            out_specs=[whole(HD, width)] * 4 + [whole(own, width)],
            scratch_shapes=[
                pltpu.VMEM((3, width, width), half),
                pltpu.SemaphoreType.DMA((3,)),
            ],
        ),
        out_shape=[jax.ShapeDtypeStruct((HD, width), full)] * 4 + [jax.ShapeDtypeStruct((own, width), full)],
        compiler_params=pltpu.CompilerParams(vmem_limit_bytes=WIDE),
    )(index, sums, w_query, w_key, w_value)


def exchange(array, axis):
    return lax.all_to_all(array, axis, split_axis=0, concat_axis=0, tiled=True)


def per_device(
    grid_fields,
    cotangent,
    encoder_source,
    encoder_target,
    encoder_count,
    mesh_source,
    mesh_target,
    mesh_count,
    w_encoder,
    w_query,
    w_key,
    w_value,
    w_output,
):
    model_size = lax.axis_size("mp")
    data_size = lax.axis_size("dp")
    model_index = lax.axis_index("mp")
    local_grid = grid_fields[0]
    local_cot = cotangent[0]
    points, channels = local_grid.shape
    node_rows, width = local_cot.shape
    nodes = node_rows * model_size
    own_channels = channels // model_size

    other = lax.ppermute(local_cot, "mp", [(i, i ^ 1) for i in range(model_size)])

    partials = encoder_partials(
        local_grid,
        encoder_source,
        encoder_target,
        encoder_count,
        (model_index * points).reshape(1).astype(jnp.int32),
        w_output,
        local_cot,
    )
    partials, mesh_count = lax.optimization_barrier((partials, mesh_count))
    received = exchange(partials, "mp")
    copies = collect(received, node_rows)
    encoded = exchange(copies, "mp")
    place = model_index.reshape(1).astype(jnp.int32)
    pairs, folded = edge_counts(
        mesh_source, mesh_target, mesh_count, place, w_encoder, w_query, w_key, w_value, nodes
    )
    pairs, other = lax.optimization_barrier((pairs, other))
    both = pair_up((model_index % 2).reshape(1).astype(jnp.int32), local_cot, other)
    lanes = [list(range(first, model_size, 2)) for first in range(2)]
    all_cot = lax.all_gather(both, "mp", axis=0, tiled=True, axis_index_groups=lanes)
    left, grads = attention(place, encoded, w_encoder, folded, received, pairs, data_size)

    packed = jnp.concatenate([grads, meet(left, all_cot, data_size, own_channels)], axis=1)
    shares = exchange(packed, "dp")
    share = jnp.sum(shares.astype(full), axis=0).astype(half)
    rows = grads.shape[1]
    met = share[None, rows:]
    share = share[:rows]
    across = [
        (data * model_size + model, data * model_size + (model + data) % model_size)
        for data in range(data_size)
        for model in range(model_size)
    ]
    swapped = lax.ppermute(share, ("dp", "mp"), across)
    sums = exchange(join(met, swapped, own_channels, data_size), "dp")
    norm = 1.0 / math.sqrt(data_size * nodes)
    return tuple(finish(place, sums, w_query, w_key, w_value, norm, own_channels))


def solution(mesh):
    in_specs = (
        P("dp", "mp", None),
        P("dp", "mp", None),
        P(),
        P(),
        P(),
        P(),
        P(),
        P(),
        P(),
        P(),
        P(),
        P(),
        P(),
    )
    out_specs = (P("mp", None), P("mp", None), P("mp", None), P("mp", None), P("mp", None))
    return jax.shard_map(
        per_device, mesh=mesh, in_specs=in_specs, out_specs=out_specs, check_vma=False
    )
```
